32 devices in a mesh: expert: 16 (over z, y, x), dp: 2 (over core).
Axes of the slice: x: 2, y: 2, z: 4, core: 2. Of those that a mesh axis runs over, the one named last changes fastest.
Arguments:
- tokens: bfloat16 [2048, 4096], P(('expert', 'dp')), may hold values from -6 to 6
- routes: int32 [2048, 8], P(('expert', 'dp')), may hold values from 0 to 15, all different within a row; in each aligned block of 64 rows (0 to 63, 64 to 127, ...) at most 64 rows name the same one
- gate_probs: float32 [2048, 8], P(('expert', 'dp')), may hold values from 0.05 to 0.35
- gate_w: bfloat16 [16, 4096, 768], P('expert', None, 'dp'), may hold values from -0.09375 to 0.09375
- up_w: bfloat16 [16, 4096, 768], P('expert', None, 'dp'), may hold values from -0.09375 to 0.09375
- down_w: bfloat16 [16, 768, 4096], P('expert', 'dp'), may hold values from -0.21875 to 0.21875
Outputs:
- mixed_out: bfloat16 [2048, 4096], P(('expert', 'dp'))
The draws below stay inside these ranges and needn't reach their ends.
Inputs may be any that keep to these rules, and one draw needn't show every extreme that they name: `routes`: each token names 8 different experts. Among the 64 tokens of one device (aligned blocks of rows), no expert is named by more than 64 tokens; in some block an expert is named by exactly 64 tokens.
All inputs are finite; a program needn't handle non-finite values.
Results may differ from the reference program's by a relative error of at most 0.0057.
Values may be sent and summed in bfloat16 or wider, within the bound.
A program may use at most 192 MiB of HBM per device.

```python
import math
import jax
import jax.numpy as jnp
import numpy as np
from jax import lax

D = 4096
HID = 768
TOP = 8
TOK_DEV = 64
EXPERTS = 16
CAP = 64
TOKENS = 2048


def level_of(key, shape, split, low, largest):
    def one(dim, shards_of):
        heights = jax.random.uniform(jax.random.fold_in(jax.random.fold_in(key, 6), dim), (shards_of,), jnp.float32, low / len(split), largest / len(split))
        return jnp.repeat(jnp.exp(heights), shape[dim] // shards_of).reshape((-1,) + (1,) * (len(shape) - dim - 1))

    loudness = one(*split[0])
    for cut in split[1:]:
        loudness = loudness * one(*cut)
    return loudness


def deal_out(key, own, number, rows, count, top, limit, lean):
    ranking = jax.random.permutation(key, count)
    heavy_load, common = shares(count, rows * top, limit, lean, True), shares(count, rows * top, limit, lean, False)
    places = jnp.arange(count)

    def named(tallies, rotation):
        used = int((tallies > 0).sum())
        fixed = max(1, used // 4)
        shifted = fixed + (places - fixed + rotation * (used - fixed)) % max(1, count - fixed)
        return jnp.zeros((count,), jnp.int32).at[ranking[jnp.where(places < fixed, places, shifted)]].set(jnp.asarray(tallies, jnp.int32))

    tallies = jnp.where(number % 4 == 0, named(heavy_load, number // 4), named(common, number - number // 4 - 1))
    mixed = jax.random.permutation(jax.random.fold_in(own, 3), count)
    donor, taker = mixed[0:count // 2 * 2:2], mixed[1:count // 2 * 2:2]
    margin = jnp.minimum(tallies[donor] - 1, limit - tallies[taker]) // 2
    margin = jnp.where((donor == ranking[0]) | (taker == ranking[0]) | (tallies[taker] == 0), 0, jnp.maximum(margin, 0))
    shifted = jax.random.randint(jax.random.fold_in(own, 4), (count // 2,), 0, 1 << 20) % (margin + 1)
    tallies = tallies.at[donor].add(-shifted).at[taker].add(shifted)
    items = jnp.searchsorted(jnp.cumsum(tallies), jnp.arange(rows * top), side="right").astype(jnp.int32)
    table = items.reshape(top, rows).T
    table = table[jax.random.permutation(jax.random.fold_in(own, 1), rows)]
    rotation = jax.random.randint(jax.random.fold_in(own, 2), (rows, 1), 0, top)
    return jnp.take_along_axis(table, (jnp.arange(top)[None, :] + rotation) % top, axis=1)


def shares(number_of, total, bound, lean, full):
    loads = [(1 << 20) // math.isqrt(standing ** lean) + 1 for standing in range(1, number_of + 1)]
    largest = bound if full else min(bound, max(-(-total // number_of), total * loads[0] // sum(loads)))
    least = 1 if total - largest >= number_of - 1 else 0
    given, spare = [largest] + [least] * (number_of - 1), total - largest - least * (number_of - 1)
    while spare > 0:
        candidates = [i for i in range(1, number_of) if given[i] < largest] or [i for i in range(1, number_of) if given[i] < bound]
        pool, remaining = sum([loads[i] for i in candidates]), spare
        for i in candidates:
            more = min(bound - given[i], max(1, remaining * loads[i] // pool), spare)
            given[i] = given[i] + more
            spare = spare - more
    return np.array(given)


def normal_values(key, dims, width, most, pieces=(), kind=jnp.bfloat16):
    entries = width * jax.random.normal(key, dims, jnp.float32)
    if pieces:
        entries = entries * level_of(key, dims, pieces, -0.22, 0.18)
    return jnp.clip(entries, -most, most).astype(kind)


def setup_inputs(seed: int = 0) -> dict:
    seeds = jax.random.split(jax.random.key(seed), 7)
    tokens = normal_values(seeds[0], (TOKENS, D), 1.0, 6.0, ((0, 32),))
    routes_keys = jax.random.split(jax.random.fold_in(seeds[1], 1), TOKENS // TOK_DEV)
    routes_turns = jax.random.permutation(jax.random.fold_in(seeds[1], 3), TOKENS // TOK_DEV)
    routes = jax.vmap(lambda own, number: deal_out(jax.random.fold_in(seeds[1], 2), own, number, TOK_DEV, EXPERTS, TOP, CAP, 2))(routes_keys, routes_turns).reshape((TOKENS, TOP))
    gate_probs = jnp.clip(0.05 + 0.29999999 * jax.random.uniform(seeds[2], (TOKENS, TOP), jnp.float32) ** level_of(seeds[2], (TOKENS, TOP), ((0, 32),), -0.2, 0.2), 0.05, 0.35)
    gate_w = normal_values(seeds[3], (EXPERTS, D, HID), D ** -0.5, 0.09375, ((0, 16), (2, 2)))
    up_w = normal_values(seeds[4], (EXPERTS, D, HID), D ** -0.5, 0.09375, ((0, 16), (2, 2)))
    down_w = normal_values(seeds[5], (EXPERTS, HID, D), HID ** -0.5, 0.21875, ((0, 16), (1, 2)))
    return dict(tokens=tokens, routes=routes, gate_probs=gate_probs, gate_w=gate_w, up_w=up_w, down_w=down_w)


def reference(tokens, routes, gate_probs, gate_w, up_w, down_w):
    device_count = TOKENS // TOK_DEV
    local_routes = routes.reshape(device_count, TOK_DEV, TOP)
    expert_ids = jnp.arange(EXPERTS, dtype=jnp.int32)
    named_hits = jnp.sum((local_routes[..., None] == expert_ids).astype(jnp.int32), axis=2)
    before = jnp.cumsum(named_hits, axis=1) - named_hits
    slot_index = jnp.take_along_axis(before, local_routes, axis=2)
    sources = jnp.arange(device_count, dtype=jnp.int32)[:, None, None]
    buffer_row = (sources * CAP + slot_index).reshape(TOKENS, TOP).astype(jnp.int32)
    token_ids = jnp.broadcast_to(jnp.arange(TOKENS, dtype=jnp.int32)[:, None], (TOKENS, TOP))
    source_table = jnp.full((EXPERTS, device_count * CAP), TOKENS, jnp.int32).at[routes, buffer_row].set(token_ids)
    weight_table = jnp.zeros((EXPERTS, device_count * CAP), jnp.float32).at[routes, buffer_row].set(gate_probs.astype(jnp.float32))
    padded = jnp.concatenate([tokens, jnp.zeros((1, D), tokens.dtype)], axis=0)

    def expert_pass(running, inputs):
        row_ids, row_weights, gate_part, up_part, down_part = inputs
        gathered = padded[row_ids]
        gate_act = jnp.dot(gathered, gate_part, preferred_element_type=jnp.float32)
        up_act = jnp.dot(gathered, up_part, preferred_element_type=jnp.float32)
        hidden = (jax.nn.silu(gate_act) * up_act).astype(jnp.bfloat16)
        expert_out = jnp.dot(hidden, down_part, preferred_element_type=jnp.float32).astype(jnp.bfloat16)
        running = running.at[row_ids].add(row_weights[:, None] * expert_out.astype(jnp.float32), mode="drop")
        return running, None

    start = jnp.zeros((TOKENS, D), jnp.float32)
    total, _ = lax.scan(expert_pass, start, (source_table, weight_table, gate_w, up_w, down_w))
    return total.astype(jnp.bfloat16)
```

```python
import jax
import jax.numpy as jnp
from jax import lax
from jax.sharding import PartitionSpec as P


def swiglu(row_block, w_gate, w_up, w_down):
    gate_act = jnp.dot(row_block, w_gate, preferred_element_type=jnp.float32)
    up_act = jnp.dot(row_block, w_up, preferred_element_type=jnp.float32)
    hidden = (jax.nn.silu(gate_act) * up_act).astype(jnp.bfloat16)
    return jnp.dot(hidden, w_down, preferred_element_type=jnp.float32)


def apply_expert(row_block, w_gate, w_up, w_down):
    return swiglu(row_block, w_gate, w_up, w_down)


def exchange_body(tokens, routes, gate_probs, gate_w, up_w, down_w):
    experts = lax.axis_size("expert")
    tok_count, model_width = tokens.shape
    top_count = routes.shape[1]
    capacity = 2 * tok_count * top_count // experts
    expert_ids = jnp.arange(experts, dtype=jnp.int32)
    named_hits = jnp.sum((routes[:, :, None] == expert_ids).astype(jnp.int32), axis=1)
    before = jnp.cumsum(named_hits, axis=0) - named_hits
    slot_index = jnp.take_along_axis(before, routes, axis=1)
    target = routes * capacity + slot_index
    buffer_rows = jnp.arange(experts * capacity, dtype=jnp.int32)
    placer = jnp.sum(
        (target[None, :, :] == buffer_rows[:, None, None]).astype(jnp.float32), axis=2
    ).astype(jnp.bfloat16)
    outgoing = jnp.dot(placer, tokens, preferred_element_type=jnp.float32).astype(jnp.bfloat16)
    outgoing = outgoing.reshape(experts, capacity, model_width)
    present = (
        jnp.sum(placer.astype(jnp.float32), axis=1).astype(jnp.bfloat16).reshape(experts, capacity)
    )
    w_gate = gate_w[0]
    w_up = up_w[0]
    w_down = down_w[0]
    row_block = lax.all_to_all(outgoing, "expert", split_axis=0, concat_axis=0, tiled=True)
    flag_block = lax.all_to_all(present, "expert", split_axis=0, concat_axis=0, tiled=True)
    source_count = row_block.shape[0]
    item_count = row_block.shape[1]
    flat_rows = row_block.reshape(-1, model_width)
    flat_flags = flag_block.reshape(-1)
    both_rows = lax.all_gather(flat_rows, "dp", axis=0, tiled=True)
    partial_out = apply_expert(both_rows, w_gate, w_up, w_down)
    result = lax.psum_scatter(partial_out, "dp", scatter_dimension=0, tiled=True)
    masked = result * flat_flags.astype(jnp.float32)[:, None]
    answered = masked.astype(jnp.bfloat16).reshape(source_count, item_count, model_width)
    returned = lax.all_to_all(answered, "expert", split_axis=0, concat_axis=0, tiled=True)
    picked = returned.reshape(experts * capacity, model_width)[target]
    mixed_out = jnp.einsum(
        "tk,tkd->td", gate_probs, picked.astype(jnp.float32), precision=lax.Precision.HIGHEST
    )
    return mixed_out.astype(jnp.bfloat16)


def gather_body(tokens, routes, gate_probs, gate_w, up_w, down_w):
    experts = lax.axis_size("expert")
    me = lax.axis_index("expert")
    expert_ids = jnp.arange(experts, dtype=jnp.int32)
    named = routes[:, :, None] == expert_ids
    spread = jnp.sum(jnp.where(named, gate_probs[:, :, None], 0.0), axis=1)
    w_gate = lax.all_gather(gate_w[0], "dp", axis=1, tiled=True)
    w_up = lax.all_gather(up_w[0], "dp", axis=1, tiled=True)
    w_down = lax.all_gather(down_w[0], "dp", axis=0, tiled=True)
    all_rows = lax.all_gather(tokens, "expert", axis=0, tiled=True)
    all_spread = lax.all_gather(spread, "expert", axis=0, tiled=True)
    weight = lax.dynamic_slice_in_dim(all_spread, me, 1, axis=1)
    out = apply_expert(all_rows, w_gate, w_up, w_down) * weight
    return lax.psum_scatter(
        out.astype(jnp.bfloat16), "expert", scatter_dimension=0, tiled=True
    )


def body(tokens, routes, *others):
    tok_count, top_count = routes.shape
    capacity = 2 * tok_count * top_count // lax.axis_size("expert")
    if capacity >= tok_count:
        return gather_body(tokens, routes, *others)
    return exchange_body(tokens, routes, *others)


def solution(mesh):
    return jax.shard_map(
        body,
        mesh=mesh,
        in_specs=(
            P(("expert", "dp"), None),
            P(("expert", "dp"), None),
            P(("expert", "dp"), None),
            P("expert", None, "dp"),
            P("expert", None, "dp"),
            P("expert", "dp", None),
        ),
        out_specs=P(("expert", "dp"), None),
        check_vma=False,
    )
```

```python
import jax
import jax.numpy as jnp
from jax import lax
from jax.experimental import pallas as pl
from jax.experimental.pallas import tpu as pltpu
from jax.sharding import PartitionSpec as P


def swiglu(row_block, w_gate, w_up, w_down):
    gate_act = jnp.dot(row_block, w_gate, preferred_element_type=jnp.float32)
    up_act = jnp.dot(row_block, w_up, preferred_element_type=jnp.float32)
    hidden = (jax.nn.silu(gate_act) * up_act).astype(jnp.bfloat16)
    return jnp.dot(hidden, w_down, preferred_element_type=jnp.float32)


def apply_expert(row_block, w_gate, w_up, w_down):
    return swiglu(row_block, w_gate, w_up, w_down)


def exchange_body(tokens, routes, gate_probs, gate_w, up_w, down_w):
    experts = lax.axis_size("expert")
    tok_count, model_width = tokens.shape
    top_count = routes.shape[1]
    capacity = 2 * tok_count * top_count // experts
    expert_ids = jnp.arange(experts, dtype=jnp.int32)
    named_hits = jnp.sum((routes[:, :, None] == expert_ids).astype(jnp.int32), axis=1)
    before = jnp.cumsum(named_hits, axis=0) - named_hits
    slot_index = jnp.take_along_axis(before, routes, axis=1)
    target = routes * capacity + slot_index
    buffer_rows = jnp.arange(experts * capacity, dtype=jnp.int32)
    placer = jnp.sum(
        (target[None, :, :] == buffer_rows[:, None, None]).astype(jnp.float32), axis=2
    ).astype(jnp.bfloat16)
    outgoing = jnp.dot(placer, tokens, preferred_element_type=jnp.float32).astype(jnp.bfloat16)
    outgoing = outgoing.reshape(experts, capacity, model_width)
    present = (
        jnp.sum(placer.astype(jnp.float32), axis=1).astype(jnp.bfloat16).reshape(experts, capacity)
    )
    w_gate = gate_w[0]
    w_up = up_w[0]
    w_down = down_w[0]
    row_block = lax.all_to_all(outgoing, "expert", split_axis=0, concat_axis=0, tiled=True)
    flag_block = lax.all_to_all(present, "expert", split_axis=0, concat_axis=0, tiled=True)
    source_count = row_block.shape[0]
    item_count = row_block.shape[1]
    flat_rows = row_block.reshape(-1, model_width)
    flat_flags = flag_block.reshape(-1)
    both_rows = lax.all_gather(flat_rows, "dp", axis=0, tiled=True)
    partial_out = apply_expert(both_rows, w_gate, w_up, w_down)
    result = lax.psum_scatter(partial_out, "dp", scatter_dimension=0, tiled=True)
    masked = result * flat_flags.astype(jnp.float32)[:, None]
    answered = masked.astype(jnp.bfloat16).reshape(source_count, item_count, model_width)
    returned = lax.all_to_all(answered, "expert", split_axis=0, concat_axis=0, tiled=True)
    picked = returned.reshape(experts * capacity, model_width)[target]
    mixed_out = jnp.einsum(
        "tk,tkd->td", gate_probs, picked.astype(jnp.float32), precision=lax.Precision.HIGHEST
    )
    return mixed_out.astype(jnp.bfloat16)


MESH = pl.DeviceIdType.MESH
DEPTH = 4
TAG = 128


def fused_kernel(
    rows_ref, gate_ref, up_ref, down_ref, out_ref,
    xa, xb, w_in, w_out, hidden, stay, pass_on, leave, got_third, got_second, rise, fall,
    gather_send, gather_recv, reduce_send, reduce_recv, weight_sem,
):
    tok = rows_ref.shape[0]
    half = xb.shape[2]
    unit = gate_ref.shape[1]
    me = lax.axis_index("expert")
    core = lax.axis_index("dp")
    z = me // 4
    y = (me // 2) % 2
    x = me % 2
    above, below = {"expert": me + 4}, {"expert": me - 4}
    across_y, across_x = {"expert": me + 2 - 4 * y}, {"expert": me + 1 - 2 * x}
    sibling = {"dp": 1 - core}
    second = (across_y, across_x)
    third = (across_x, across_y)
    feats = (xa, xb)

    def when(cond, fn):
        pl.when(cond)(fn)

    def piece(zz):
        if isinstance(zz, int):
            return pl.ds(zz * tok, tok)
        return pl.ds(pl.multiple_of(zz * tok, tok), tok)

    def remote(src, dst, send, recv, device):
        return pltpu.make_async_remote_copy(
            src_ref=src, dst_ref=dst, send_sem=send, recv_sem=recv,
            device_id=device, device_id_type=MESH,
        )

    barrier = pltpu.get_barrier_semaphore()
    for device in (across_y, across_x, sibling):
        pl.semaphore_signal(barrier, inc=1, device_id=device, device_id_type=MESH)

    @pl.when(z < DEPTH - 1)
    def _():
        pl.semaphore_signal(barrier, inc=1, device_id=above, device_id_type=MESH)

    @pl.when(z > 0)
    def _():
        pl.semaphore_signal(barrier, inc=1, device_id=below, device_id_type=MESH)

    xa[0, piece(z), :] = rows_ref[:, : TAG + half]
    xb[0, piece(z), :] = rows_ref[:, TAG + half :]

    edge = jnp.logical_or(z == 0, z == DEPTH - 1)

    @pl.when(edge)
    def _():
        pl.semaphore_wait(barrier, 4)

    @pl.when(jnp.logical_not(edge))
    def _():
        pl.semaphore_wait(barrier, 5)

    def gather(f, src_kind, dst_kind, zz, slot, device):
        return remote(
            feats[f].at[src_kind, piece(zz)], feats[f].at[dst_kind, piece(zz)],
            gather_send.at[f, slot + zz], gather_recv.at[f, dst_kind * DEPTH + zz], device,
        )

    def climb(f, zz):
        return gather(f, 0, 0, zz, 0, above)

    def sink(f, zz):
        return gather(f, 0, 0, zz, 4, below)

    def own_second(f, zz):
        return gather(f, 0, 1, zz, 8, second[f])

    def own_third(f, zz):
        return gather(f, 0, 2, zz, 12, third[f])

    def second_third(f, zz):
        return gather(f, 1, 3, zz, 16, third[f])

    for f in range(2):
        when(z < DEPTH - 1, lambda f=f: climb(f, z).start())
        when(z > 0, lambda f=f: sink(f, z).start())
        own_second(f, z).start()
    for f in range(2):
        own_third(f, z).start()

    pairs = (
        (gate_ref, w_in.at[:, pl.ds(0, unit)], w_in.at[:, pl.ds(unit, unit)]),
        (up_ref, w_in.at[:, pl.ds(2 * unit, unit)], w_in.at[:, pl.ds(3 * unit, unit)]),
        (down_ref, w_out.at[pl.ds(0, unit)], w_out.at[pl.ds(unit, unit)]),
    )
    swaps = []
    for i, (src, mine, other) in enumerate(pairs):
        local = pltpu.make_async_copy(src, mine, weight_sem.at[3 * i])
        swap = remote(src, other, weight_sem.at[3 * i + 1], weight_sem.at[3 * i + 2], sibling)
        local.start()
        swap.start()
        swaps.append((local, swap))

    def relay_second(zz):
        for f in range(2):
            own_second(f, zz).wait_recv()
            second_third(f, zz).start()

    for k in range(1, DEPTH):
        def from_below(k=k):
            zz = z - k
            for f in range(2):
                climb(f, zz).wait_recv()
                when(z < DEPTH - 1, lambda f=f: climb(f, zz).start())
                own_second(f, zz).start()
                own_third(f, zz).start()

        def from_above(k=k):
            zz = z + k
            for f in range(2):
                sink(f, zz).wait_recv()
                when(z > 0, lambda f=f: sink(f, zz).start())
                own_second(f, zz).start()
                own_third(f, zz).start()

        when(z >= k, from_below)
        when(z + k < DEPTH, from_above)
        if k == 1:
            relay_second(z)
        else:
            when(z >= k - 1, lambda k=k: relay_second(z - k + 1))
            when(z + k - 1 < DEPTH, lambda k=k: relay_second(z + k - 1))

    def expert(kind_a, kind_b, targets):
        lane = lax.broadcasted_iota(jnp.int32, (DEPTH * tok, TAG), 1)
        mine = jnp.logical_or(lane == me, lane == me + 16)
        tags = xa[kind_a, :, :TAG].astype(jnp.float32)
        weight = jnp.sum(jnp.where(mine, tags, 0.0), axis=1, keepdims=True)

        def hidden_tile(j, carry):
            cols = pl.multiple_of(j * 256, 256)
            gate_cols, up_cols = pl.ds(cols, 256), pl.ds(2 * unit + cols, 256)

            def project(columns):
                return jnp.dot(
                    xa[kind_a, :, TAG:], w_in[:half, columns], preferred_element_type=jnp.float32
                ) + jnp.dot(
                    xb[kind_b], w_in[half:, columns], preferred_element_type=jnp.float32
                )

            gate_act = project(gate_cols)
            up_act = project(up_cols)
            act = gate_act / (1.0 + jnp.exp(-gate_act)) * up_act
            hidden[:, gate_cols] = act.astype(jnp.bfloat16)
            return carry

        lax.fori_loop(0, 2 * unit // 256, hidden_tile, 0)
        for f in range(2):
            target = targets[f]

            def out_tile(j, carry, f=f, target=target):
                cols = pl.multiple_of(j * 512, 512)
                val = jnp.dot(
                    hidden[...], w_out[:, pl.ds(f * half + cols, 512)],
                    preferred_element_type=jnp.float32,
                )
                target[:, pl.ds(cols, 512)] = (val * weight).astype(target.dtype)
                return carry

            lax.fori_loop(0, half // 512, out_tile, 0)

    order = (3, 0, 2, 1)

    def leave_third(f, zz):
        return remote(
            leave.at[f, 0, piece(zz)], got_third.at[f, 0, piece(zz)],
            reduce_send.at[f, zz], reduce_recv.at[f, zz], third[f],
        )

    def leave_both(f, zz):
        return remote(
            leave.at[f, 1, piece(zz)], got_third.at[f, 1, piece(zz)],
            reduce_send.at[f, 4 + zz], reduce_recv.at[f, 4 + zz], third[f],
        )

    def leave_second(f, zz):
        return remote(
            got_third.at[f, 1, piece(zz)], got_second.at[f, piece(zz)],
            reduce_send.at[f, 8 + zz], reduce_recv.at[f, 8 + zz], second[f],
        )

    def rising(f, zz):
        return remote(
            rise.at[f, piece(zz)], rise.at[f, piece(zz)],
            reduce_send.at[f, 12 + zz], reduce_recv.at[f, 12 + zz], above,
        )

    def falling(f, zz):
        return remote(
            fall.at[f, piece(zz)], fall.at[f, piece(zz)],
            reduce_send.at[f, 16 + zz], reduce_recv.at[f, 16 + zz], below,
        )

    for local, swap in swaps:
        local.wait()
        swap.wait_recv()
    expert(0, 0, (stay.at[0], stay.at[1]))
    when(z >= 3, lambda: relay_second(z - 3))
    when(z + 3 < DEPTH, lambda: relay_second(z + 3))

    for zz in range(DEPTH):
        own_third(0, zz).wait_recv()
    expert(2, 1, (leave.at[0, 0], pass_on.at[1]))
    for zz in order:
        leave_third(0, zz).start()
    for zz in range(DEPTH):
        own_third(1, zz).wait_recv()
    expert(1, 2, (pass_on.at[0], leave.at[1, 0]))
    for zz in order:
        leave_third(1, zz).start()
    for zz in range(DEPTH):
        for f in range(2):
            second_third(f, zz).wait_recv()
    expert(3, 3, (leave.at[0, 1], leave.at[1, 1]))
    for zz in order:
        for f in range(2):
            leave_both(f, zz).start()

    def wide(ref):
        return ref.astype(jnp.float32)

    def to_second(zz):
        for f in range(2):
            leave_both(f, zz).wait_recv()
            val = pass_on[f, piece(zz), :] + wide(got_third[f, 1, piece(zz), :])
            got_third[f, 1, piece(zz), :] = val.astype(jnp.bfloat16)
            leave_second(f, zz).start()

    def settle(zz):
        for f in range(2):
            leave_third(f, zz).wait_recv()
            leave_second(f, zz).wait_recv()
            stay[f, piece(zz), :] = (
                stay[f, piece(zz), :]
                + wide(got_third[f, 0, piece(zz), :])
                + wide(got_second[f, piece(zz), :])
            )

        def first_up():
            for f in range(2):
                rise[f, piece(zz), :] = stay[f, piece(zz), :].astype(jnp.bfloat16)
                rising(f, zz).start()

        def first_down():
            for f in range(2):
                fall[f, piece(zz), :] = stay[f, piece(zz), :].astype(jnp.bfloat16)
                falling(f, zz).start()

        if zz > 0:
            when(z == 0, first_up)
        if zz < DEPTH - 1:
            when(z == DEPTH - 1, first_down)

    def relay_up(zz):
        for f in range(2):
            rising(f, zz).wait_recv()
            val = stay[f, piece(zz), :] + wide(rise[f, piece(zz), :])
            rise[f, piece(zz), :] = val.astype(jnp.bfloat16)
            rising(f, zz).start()

    def relay_down(zz):
        for f in range(2):
            falling(f, zz).wait_recv()
            val = stay[f, piece(zz), :] + wide(fall[f, piece(zz), :])
            fall[f, piece(zz), :] = val.astype(jnp.bfloat16)
            falling(f, zz).start()

    to_second(order[0])
    for i in range(1, DEPTH + 1):
        if i < DEPTH:
            to_second(order[i])
        settle(order[i - 1])
        if i == 2:
            when(z == 1, lambda: relay_up(3))
            when(z == 2, lambda: relay_down(0))
        if i == 3:
            when(z == 1, lambda: relay_down(0))
            when(z == 2, lambda: relay_up(3))
    when(z == 1, lambda: relay_up(2))
    when(z == 2, lambda: relay_down(1))

    cols = (pl.ds(0, half), pl.ds(half, half))

    def finish(up, down):
        for f in range(2):
            val = stay[f, piece(z), :]
            if up:
                rising(f, z).wait_recv()
                val = val + wide(rise[f, piece(z), :])
            if down:
                falling(f, z).wait_recv()
                val = val + wide(fall[f, piece(z), :])
            out_ref[:, cols[f]] = val.astype(out_ref.dtype)

    when(z == 0, lambda: finish(False, True))
    when(z == DEPTH - 1, lambda: finish(True, False))
    when(jnp.logical_not(edge), lambda: finish(True, True))

    for _, swap in swaps:
        swap.wait_send()
    for f in range(2):
        for zz in range(DEPTH):
            when(jnp.logical_and(z < DEPTH - 1, zz <= z), lambda f=f, zz=zz: climb(f, zz).wait_send())
            when(jnp.logical_and(z > 0, zz >= z), lambda f=f, zz=zz: sink(f, zz).wait_send())
            for copy in (own_second, own_third, second_third, leave_third, leave_both, leave_second):
                copy(f, zz).wait_send()
            when(zz > z, lambda f=f, zz=zz: rising(f, zz).wait_send())
            when(zz < z, lambda f=f, zz=zz: falling(f, zz).wait_send())


def fused_body(tokens, routes, gate_probs, gate_w, up_w, down_w):
    experts = lax.axis_size("expert")
    tok, width = tokens.shape
    unit = gate_w.shape[2]
    half = width // 2
    line = DEPTH * tok
    expert_ids = jnp.arange(experts, dtype=jnp.int32)
    named = routes[:, :, None] == expert_ids
    spread = jnp.sum(jnp.where(named, gate_probs[:, :, None], 0.0), axis=1)
    coarse = lax.reduce_precision(spread, 8, 7)
    fine = spread - coarse
    tags = jnp.concatenate([coarse, fine], axis=1).astype(jnp.bfloat16)
    tags = jnp.pad(tags, ((0, 0), (0, TAG - 2 * experts)))
    rows = jnp.concatenate([tags, tokens], axis=1)
    vmem, anywhere = pl.BlockSpec(memory_space=pltpu.VMEM), pl.BlockSpec(memory_space=pl.ANY)
    bf16, f32, dma = jnp.bfloat16, jnp.float32, pltpu.SemaphoreType.DMA
    return pl.pallas_call(
        fused_kernel,
        out_shape=jax.ShapeDtypeStruct((tok, width), bf16),
        in_specs=[vmem, anywhere, anywhere, anywhere],
        out_specs=vmem,
        scratch_shapes=[
            pltpu.VMEM((4, line, TAG + half), bf16),
            pltpu.VMEM((4, line, half), bf16),
            pltpu.VMEM((width, 4 * unit), bf16),
            pltpu.VMEM((2 * unit, width), bf16),
            pltpu.VMEM((line, 2 * unit), bf16),
            pltpu.VMEM((2, line, half), f32),
            pltpu.VMEM((2, line, half), f32),
            pltpu.VMEM((2, 2, line, half), bf16),
            pltpu.VMEM((2, 2, line, half), bf16),
            pltpu.VMEM((2, line, half), bf16),
            pltpu.VMEM((2, line, half), bf16),
            pltpu.VMEM((2, line, half), bf16),
            dma((2, 20)),
            dma((2, 16)),
            dma((2, 20)),
            dma((2, 20)),
            dma((9,)),
        ],
        compiler_params=pltpu.CompilerParams(
            collective_id=0, has_side_effects=True, vmem_limit_bytes=60 * 2**20
        ),
        cost_estimate=pl.CostEstimate(
            flops=2 * experts * tok * width * unit * 6,
            bytes_accessed=6 * width * unit * 2,
            transcendentals=experts * tok * unit * 2,
        ),
    )(rows, gate_w[0], up_w[0], down_w[0])


def body(tokens, routes, *others):
    tok_count, top_count = routes.shape
    experts = lax.axis_size("expert")
    capacity = 2 * tok_count * top_count // experts
    if capacity >= tok_count and experts == 4 * DEPTH and lax.axis_size("dp") == 2:
        return fused_body(tokens, routes, *others)
    return exchange_body(tokens, routes, *others)


def solution(mesh):
    return jax.shard_map(
        body,
        mesh=mesh,
        in_specs=(
            P(("expert", "dp"), None),
            P(("expert", "dp"), None),
            P(("expert", "dp"), None),
            P("expert", None, "dp"),
            P("expert", None, "dp"),
            P("expert", "dp", None),
        ),
        out_specs=P(("expert", "dp"), None),
        check_vma=False,
    )
```

```python
import jax
import jax.numpy as jnp
from jax import lax
from jax.experimental import pallas as pl
from jax.experimental.pallas import tpu as pltpu
from jax.sharding import PartitionSpec as P


def swiglu(row_block, w_gate, w_up, w_down):
    gate_act = jnp.dot(row_block, w_gate, preferred_element_type=jnp.float32)
    up_act = jnp.dot(row_block, w_up, preferred_element_type=jnp.float32)
    hidden = (jax.nn.silu(gate_act) * up_act).astype(jnp.bfloat16)
    return jnp.dot(hidden, w_down, preferred_element_type=jnp.float32)


def apply_expert(row_block, w_gate, w_up, w_down):
    return swiglu(row_block, w_gate, w_up, w_down)


def exchange_body(tokens, routes, gate_probs, gate_w, up_w, down_w):
    experts = lax.axis_size("expert")
    tok_count, model_width = tokens.shape
    top_count = routes.shape[1]
    capacity = 2 * tok_count * top_count // experts
    expert_ids = jnp.arange(experts, dtype=jnp.int32)
    named_hits = jnp.sum((routes[:, :, None] == expert_ids).astype(jnp.int32), axis=1)
    before = jnp.cumsum(named_hits, axis=0) - named_hits
    slot_index = jnp.take_along_axis(before, routes, axis=1)
    target = routes * capacity + slot_index
    buffer_rows = jnp.arange(experts * capacity, dtype=jnp.int32)
    placer = jnp.sum(
        (target[None, :, :] == buffer_rows[:, None, None]).astype(jnp.float32), axis=2
    ).astype(jnp.bfloat16)
    outgoing = jnp.dot(placer, tokens, preferred_element_type=jnp.float32).astype(jnp.bfloat16)
    outgoing = outgoing.reshape(experts, capacity, model_width)
    present = (
        jnp.sum(placer.astype(jnp.float32), axis=1).astype(jnp.bfloat16).reshape(experts, capacity)
    )
    w_gate = gate_w[0]
    w_up = up_w[0]
    w_down = down_w[0]
    row_block = lax.all_to_all(outgoing, "expert", split_axis=0, concat_axis=0, tiled=True)
    flag_block = lax.all_to_all(present, "expert", split_axis=0, concat_axis=0, tiled=True)
    source_count = row_block.shape[0]
    item_count = row_block.shape[1]
    flat_rows = row_block.reshape(-1, model_width)
    flat_flags = flag_block.reshape(-1)
    both_rows = lax.all_gather(flat_rows, "dp", axis=0, tiled=True)
    partial_out = apply_expert(both_rows, w_gate, w_up, w_down)
    result = lax.psum_scatter(partial_out, "dp", scatter_dimension=0, tiled=True)
    masked = result * flat_flags.astype(jnp.float32)[:, None]
    answered = masked.astype(jnp.bfloat16).reshape(source_count, item_count, model_width)
    returned = lax.all_to_all(answered, "expert", split_axis=0, concat_axis=0, tiled=True)
    picked = returned.reshape(experts * capacity, model_width)[target]
    mixed_out = jnp.einsum(
        "tk,tkd->td", gate_probs, picked.astype(jnp.float32), precision=lax.Precision.HIGHEST
    )
    return mixed_out.astype(jnp.bfloat16)


MESH = pl.DeviceIdType.MESH
DEPTH = 4
TAG = 128


def fused_kernel(
    rows_ref, routes_ref, probs_ref, gate_ref, up_ref, down_ref, out_ref,
    xa, xb, w_in, w_out, hidden, stay, pass_on, leave, got_third, got_second, rise, fall,
    gather_send, gather_recv, reduce_send, reduce_recv, weight_sem,
):
    tok = rows_ref.shape[0]
    half = xb.shape[2]
    unit = gate_ref.shape[1]
    me = lax.axis_index("expert")
    core = lax.axis_index("dp")
    z = me // 4
    y = (me // 2) % 2
    x = me % 2
    above, below = {"expert": me + 4}, {"expert": me - 4}
    across_y, across_x = {"expert": me + 2 - 4 * y}, {"expert": me + 1 - 2 * x}
    sibling = {"dp": 1 - core}
    second = (across_y, across_x)
    third = (across_x, across_y)
    feats = (xa, xb)

    def when(cond, fn):
        pl.when(cond)(fn)

    def piece(zz):
        if isinstance(zz, int):
            return pl.ds(zz * tok, tok)
        return pl.ds(pl.multiple_of(zz * tok, tok), tok)

    def remote(src, dst, send, recv, device):
        return pltpu.make_async_remote_copy(
            src_ref=src, dst_ref=dst, send_sem=send, recv_sem=recv,
            device_id=device, device_id_type=MESH,
        )

    barrier = pltpu.get_barrier_semaphore()
    for device in (across_y, across_x, sibling):
        pl.semaphore_signal(barrier, inc=1, device_id=device, device_id_type=MESH)

    @pl.when(z < DEPTH - 1)
    def _():
        pl.semaphore_signal(barrier, inc=1, device_id=above, device_id_type=MESH)

    @pl.when(z > 0)
    def _():
        pl.semaphore_signal(barrier, inc=1, device_id=below, device_id_type=MESH)

    tag_lane = lax.broadcasted_iota(jnp.int32, (tok, TAG), 1)
    spread = jnp.zeros((tok, TAG), jnp.float32)
    for k in range(routes_ref.shape[1]):
        named = (tag_lane & 15) == routes_ref[:, k : k + 1]
        spread = spread + jnp.where(named, probs_ref[:, k : k + 1], 0.0)
    coarse = spread.astype(jnp.bfloat16).astype(jnp.float32)
    tags_own = jnp.where(tag_lane < 16, coarse, spread - coarse)
    xa[0, piece(z), :TAG] = tags_own.astype(jnp.bfloat16)
    xa[0, piece(z), TAG:] = rows_ref[:, :half]
    xb[0, piece(z), :] = rows_ref[:, half:]

    edge = jnp.logical_or(z == 0, z == DEPTH - 1)

    @pl.when(edge)
    def _():
        pl.semaphore_wait(barrier, 4)

    @pl.when(jnp.logical_not(edge))
    def _():
        pl.semaphore_wait(barrier, 5)

    def gather(f, src_kind, dst_kind, zz, slot, device):
        return remote(
            feats[f].at[src_kind, piece(zz)], feats[f].at[dst_kind, piece(zz)],
            gather_send.at[f, slot + zz], gather_recv.at[f, dst_kind * DEPTH + zz], device,
        )

    def climb(f, zz):
        return gather(f, 0, 0, zz, 0, above)

    def sink(f, zz):
        return gather(f, 0, 0, zz, 4, below)

    def own_second(f, zz):
        return gather(f, 0, 1, zz, 8, second[f])

    def own_third(f, zz):
        return gather(f, 0, 2, zz, 12, third[f])

    def second_third(f, zz):
        return gather(f, 1, 3, zz, 16, third[f])

    for f in range(2):
        when(z < DEPTH - 1, lambda f=f: climb(f, z).start())
        when(z > 0, lambda f=f: sink(f, z).start())
        own_second(f, z).start()
    for f in range(2):
        own_third(f, z).start()

    pairs = (
        (gate_ref, w_in.at[:, pl.ds(0, unit)], w_in.at[:, pl.ds(unit, unit)]),
        (up_ref, w_in.at[:, pl.ds(2 * unit, unit)], w_in.at[:, pl.ds(3 * unit, unit)]),
        (down_ref, w_out.at[pl.ds(0, unit)], w_out.at[pl.ds(unit, unit)]),
    )
    swaps = []
    for i, (src, mine, other) in enumerate(pairs):
        local = pltpu.make_async_copy(src, mine, weight_sem.at[3 * i])
        swap = remote(src, other, weight_sem.at[3 * i + 1], weight_sem.at[3 * i + 2], sibling)
        local.start()
        swap.start()
        swaps.append((local, swap))

    def relay_second(zz):
        for f in range(2):
            own_second(f, zz).wait_recv()
            second_third(f, zz).start()

    def send_third(zz):
        for f in range(2):
            own_third(f, zz).start()

    def at_stage(k, fn):
        if k == 0:
            fn(z)
        else:
            when(z >= k, lambda: fn(z - k))
            when(z + k < DEPTH, lambda: fn(z + k))

    for k in range(1, DEPTH):
        def from_below(k=k):
            zz = z - k
            for f in range(2):
                climb(f, zz).wait_recv()
                when(z < DEPTH - 1, lambda f=f: climb(f, zz).start())
                own_second(f, zz).start()

        def from_above(k=k):
            zz = z + k
            for f in range(2):
                sink(f, zz).wait_recv()
                when(z > 0, lambda f=f: sink(f, zz).start())
                own_second(f, zz).start()

        when(z >= k, from_below)
        when(z + k < DEPTH, from_above)
        at_stage(k - 1, relay_second)
        if k == 2:
            at_stage(1, send_third)

    def expert(kind_a, kind_b, targets):
        lane = lax.broadcasted_iota(jnp.int32, (DEPTH * tok, TAG), 1)
        mine = jnp.logical_or(lane == me, lane == me + 16)
        tags = xa[kind_a, :, :TAG].astype(jnp.float32)
        weight = jnp.sum(jnp.where(mine, tags, 0.0), axis=1, keepdims=True)

        def hidden_tile(j, carry):
            cols = pl.multiple_of(j * 256, 256)
            gate_cols, up_cols = pl.ds(cols, 256), pl.ds(2 * unit + cols, 256)

            def project(columns):
                return jnp.dot(
                    xa[kind_a, :, TAG:], w_in[:half, columns], preferred_element_type=jnp.float32
                ) + jnp.dot(
                    xb[kind_b], w_in[half:, columns], preferred_element_type=jnp.float32
                )

            gate_act = project(gate_cols)
            up_act = project(up_cols)
            act = gate_act / (1.0 + jnp.exp(-gate_act)) * up_act
            hidden[:, gate_cols] = act.astype(jnp.bfloat16)
            return carry

        lax.fori_loop(0, 2 * unit // 256, hidden_tile, 0)
        for f in range(2):
            target = targets[f]

            def out_tile(j, carry, f=f, target=target):
                cols = pl.multiple_of(j * 512, 512)
                val = jnp.dot(
                    hidden[...], w_out[:, pl.ds(f * half + cols, 512)],
                    preferred_element_type=jnp.float32,
                )
                target[:, pl.ds(cols, 512)] = (val * weight).astype(target.dtype)
                return carry

            lax.fori_loop(0, half // 512, out_tile, 0)

    order = (3, 0, 2, 1)

    def leave_third(f, zz):
        return remote(
            leave.at[f, 0, piece(zz)], got_third.at[f, 0, piece(zz)],
            reduce_send.at[f, zz], reduce_recv.at[f, zz], third[f],
        )

    def leave_both(f, zz):
        return remote(
            leave.at[f, 1, piece(zz)], got_third.at[f, 1, piece(zz)],
            reduce_send.at[f, 4 + zz], reduce_recv.at[f, 4 + zz], third[f],
        )

    def leave_second(f, zz):
        return remote(
            got_third.at[f, 1, piece(zz)], got_second.at[f, piece(zz)],
            reduce_send.at[f, 8 + zz], reduce_recv.at[f, 8 + zz], second[f],
        )

    def rising(f, zz):
        return remote(
            rise.at[f, piece(zz)], rise.at[f, piece(zz)],
            reduce_send.at[f, 12 + zz], reduce_recv.at[f, 12 + zz], above,
        )

    def falling(f, zz):
        return remote(
            fall.at[f, piece(zz)], fall.at[f, piece(zz)],
            reduce_send.at[f, 16 + zz], reduce_recv.at[f, 16 + zz], below,
        )

    for local, swap in swaps:
        local.wait()
        swap.wait_recv()
    expert(0, 0, (stay.at[0], stay.at[1]))
    at_stage(3, relay_second)
    at_stage(2, send_third)
    at_stage(3, send_third)

    def wide(ref):
        return ref.astype(jnp.float32)

    def to_second(f, zz):
        leave_both(f, zz).wait_recv()
        val = pass_on[f, piece(zz), :] + wide(got_third[f, 1, piece(zz), :])
        got_third[f, 1, piece(zz), :] = val.astype(jnp.bfloat16)
        leave_second(f, zz).start()

    for zz in range(DEPTH):
        for f in range(2):
            second_third(f, zz).wait_recv()
    expert(3, 3, (leave.at[0, 1], leave.at[1, 1]))
    for zz in order:
        for f in range(2):
            leave_both(f, zz).start()

    for zz in range(DEPTH):
        own_third(0, zz).wait_recv()
    expert(2, 1, (leave.at[0, 0], pass_on.at[1]))
    for zz in order[:2]:
        to_second(1, zz)
    for zz in order:
        leave_third(0, zz).start()
    for zz in range(DEPTH):
        own_third(1, zz).wait_recv()
    expert(1, 2, (pass_on.at[0], leave.at[1, 0]))
    for zz in order[:2]:
        to_second(0, zz)
    for zz in order:
        leave_third(1, zz).start()
    for zz in order[2:]:
        for f in range(2):
            to_second(f, zz)

    def settle(zz):
        for f in range(2):
            leave_third(f, zz).wait_recv()
            leave_second(f, zz).wait_recv()
            stay[f, piece(zz), :] = (
                stay[f, piece(zz), :]
                + wide(got_third[f, 0, piece(zz), :])
                + wide(got_second[f, piece(zz), :])
            )

        def first_up():
            for f in range(2):
                rise[f, piece(zz), :] = stay[f, piece(zz), :].astype(jnp.bfloat16)
                rising(f, zz).start()

        def first_down():
            for f in range(2):
                fall[f, piece(zz), :] = stay[f, piece(zz), :].astype(jnp.bfloat16)
                falling(f, zz).start()

        if zz > 0:
            when(z == 0, first_up)
        if zz < DEPTH - 1:
            when(z == DEPTH - 1, first_down)

    def relay_up(zz):
        for f in range(2):
            rising(f, zz).wait_recv()
            val = stay[f, piece(zz), :] + wide(rise[f, piece(zz), :])
            rise[f, piece(zz), :] = val.astype(jnp.bfloat16)
            rising(f, zz).start()

    def relay_down(zz):
        for f in range(2):
            falling(f, zz).wait_recv()
            val = stay[f, piece(zz), :] + wide(fall[f, piece(zz), :])
            fall[f, piece(zz), :] = val.astype(jnp.bfloat16)
            falling(f, zz).start()

    for i in range(1, DEPTH + 1):
        settle(order[i - 1])
        if i == 2:
            when(z == 1, lambda: relay_up(3))
            when(z == 2, lambda: relay_down(0))
        if i == 3:
            when(z == 1, lambda: relay_down(0))
            when(z == 2, lambda: relay_up(3))
    when(z == 1, lambda: relay_up(2))
    when(z == 2, lambda: relay_down(1))

    cols = (pl.ds(0, half), pl.ds(half, half))

    def finish(up, down):
        for f in range(2):
            val = stay[f, piece(z), :]
            if up:
                rising(f, z).wait_recv()
                val = val + wide(rise[f, piece(z), :])
            if down:
                falling(f, z).wait_recv()
                val = val + wide(fall[f, piece(z), :])
            out_ref[:, cols[f]] = val.astype(out_ref.dtype)

    when(z == 0, lambda: finish(False, True))
    when(z == DEPTH - 1, lambda: finish(True, False))
    when(jnp.logical_not(edge), lambda: finish(True, True))

    for _, swap in swaps:
        swap.wait_send()
    for f in range(2):
        for zz in range(DEPTH):
            when(jnp.logical_and(z < DEPTH - 1, zz <= z), lambda f=f, zz=zz: climb(f, zz).wait_send())
            when(jnp.logical_and(z > 0, zz >= z), lambda f=f, zz=zz: sink(f, zz).wait_send())
            for copy in (own_second, own_third, second_third, leave_third, leave_both, leave_second):
                copy(f, zz).wait_send()
            when(zz > z, lambda f=f, zz=zz: rising(f, zz).wait_send())
            when(zz < z, lambda f=f, zz=zz: falling(f, zz).wait_send())


def fused_body(tokens, routes, gate_probs, gate_w, up_w, down_w):
    experts = lax.axis_size("expert")
    tok, width = tokens.shape
    unit = gate_w.shape[2]
    half = width // 2
    line = DEPTH * tok
    vmem, anywhere = pl.BlockSpec(memory_space=pltpu.VMEM), pl.BlockSpec(memory_space=pl.ANY)
    bf16, f32, dma = jnp.bfloat16, jnp.float32, pltpu.SemaphoreType.DMA
    return pl.pallas_call(
        fused_kernel,
        out_shape=jax.ShapeDtypeStruct((tok, width), bf16),
        in_specs=[vmem, vmem, vmem, anywhere, anywhere, anywhere],
        out_specs=vmem,
        scratch_shapes=[
            pltpu.VMEM((4, line, TAG + half), bf16),
            pltpu.VMEM((4, line, half), bf16),
            pltpu.VMEM((width, 4 * unit), bf16),
            pltpu.VMEM((2 * unit, width), bf16),
            pltpu.VMEM((line, 2 * unit), bf16),
            pltpu.VMEM((2, line, half), f32),
            pltpu.VMEM((2, line, half), f32),
            pltpu.VMEM((2, 2, line, half), bf16),
            pltpu.VMEM((2, 2, line, half), bf16),
            pltpu.VMEM((2, line, half), bf16),
            pltpu.VMEM((2, line, half), bf16),
            pltpu.VMEM((2, line, half), bf16),
            dma((2, 20)),
            dma((2, 16)),
            dma((2, 20)),
            dma((2, 20)),
            dma((9,)),
        ],
        compiler_params=pltpu.CompilerParams(
            collective_id=0, has_side_effects=True, vmem_limit_bytes=60 * 2**20
        ),
        cost_estimate=pl.CostEstimate(
            flops=2 * experts * tok * width * unit * 6,
            bytes_accessed=6 * width * unit * 2,
            transcendentals=experts * tok * unit * 2,
        ),
    )(tokens, routes, gate_probs, gate_w[0], up_w[0], down_w[0])


def body(tokens, routes, *others):
    tok_count, top_count = routes.shape
    experts = lax.axis_size("expert")
    capacity = 2 * tok_count * top_count // experts
    if capacity >= tok_count and experts == 4 * DEPTH and lax.axis_size("dp") == 2:
        return fused_body(tokens, routes, *others)
    return exchange_body(tokens, routes, *others)


def solution(mesh):
    return jax.shard_map(
        body,
        mesh=mesh,
        in_specs=(
            P(("expert", "dp"), None),
            P(("expert", "dp"), None),
            P(("expert", "dp"), None),
            P("expert", None, "dp"),
            P("expert", None, "dp"),
            P("expert", "dp", None),
        ),
        out_specs=P(("expert", "dp"), None),
        check_vma=False,
    )
```

```python
import jax
import jax.numpy as jnp
from jax import lax
from jax.experimental import pallas as pl
from jax.experimental.pallas import tpu as pltpu
from jax.sharding import PartitionSpec as P


def swiglu(row_block, w_gate, w_up, w_down):
    gate_act = jnp.dot(row_block, w_gate, preferred_element_type=jnp.float32)
    up_act = jnp.dot(row_block, w_up, preferred_element_type=jnp.float32)
    hidden = (jax.nn.silu(gate_act) * up_act).astype(jnp.bfloat16)
    return jnp.dot(hidden, w_down, preferred_element_type=jnp.float32)


def apply_expert(row_block, w_gate, w_up, w_down):
    return swiglu(row_block, w_gate, w_up, w_down)


def exchange_body(tokens, routes, gate_probs, gate_w, up_w, down_w):
    experts = lax.axis_size("expert")
    tok_count, model_width = tokens.shape
    top_count = routes.shape[1]
    capacity = 2 * tok_count * top_count // experts
    expert_ids = jnp.arange(experts, dtype=jnp.int32)
    named_hits = jnp.sum((routes[:, :, None] == expert_ids).astype(jnp.int32), axis=1)
    before = jnp.cumsum(named_hits, axis=0) - named_hits
    slot_index = jnp.take_along_axis(before, routes, axis=1)
    target = routes * capacity + slot_index
    buffer_rows = jnp.arange(experts * capacity, dtype=jnp.int32)
    placer = jnp.sum(
        (target[None, :, :] == buffer_rows[:, None, None]).astype(jnp.float32), axis=2
    ).astype(jnp.bfloat16)
    outgoing = jnp.dot(placer, tokens, preferred_element_type=jnp.float32).astype(jnp.bfloat16)
    outgoing = outgoing.reshape(experts, capacity, model_width)
    present = (
        jnp.sum(placer.astype(jnp.float32), axis=1).astype(jnp.bfloat16).reshape(experts, capacity)
    )
    w_gate = gate_w[0]
    w_up = up_w[0]
    w_down = down_w[0]
    row_block = lax.all_to_all(outgoing, "expert", split_axis=0, concat_axis=0, tiled=True)
    flag_block = lax.all_to_all(present, "expert", split_axis=0, concat_axis=0, tiled=True)
    source_count = row_block.shape[0]
    item_count = row_block.shape[1]
    flat_rows = row_block.reshape(-1, model_width)
    flat_flags = flag_block.reshape(-1)
    both_rows = lax.all_gather(flat_rows, "dp", axis=0, tiled=True)
    partial_out = apply_expert(both_rows, w_gate, w_up, w_down)
    result = lax.psum_scatter(partial_out, "dp", scatter_dimension=0, tiled=True)
    masked = result * flat_flags.astype(jnp.float32)[:, None]
    answered = masked.astype(jnp.bfloat16).reshape(source_count, item_count, model_width)
    returned = lax.all_to_all(answered, "expert", split_axis=0, concat_axis=0, tiled=True)
    picked = returned.reshape(experts * capacity, model_width)[target]
    mixed_out = jnp.einsum(
        "tk,tkd->td", gate_probs, picked.astype(jnp.float32), precision=lax.Precision.HIGHEST
    )
    return mixed_out.astype(jnp.bfloat16)


MESH = pl.DeviceIdType.MESH
DEPTH = 4
TAG = 128


def fused_kernel(
    rows_ref, tags_ref, gate_ref, up_ref, down_ref, out_ref,
    xa, xb, w_in, w_out, hidden, stay, pass_on, leave, got_third, got_second, rise, fall, early_rise, early_fall,
    gather_send, gather_recv, reduce_send, reduce_recv, weight_sem,
):
    tok = rows_ref.shape[0]
    half = xb.shape[2]
    unit = gate_ref.shape[1]
    me = lax.axis_index("expert")
    core = lax.axis_index("dp")
    z = me // 4
    y = (me // 2) % 2
    x = me % 2
    above, below = {"expert": me + 4}, {"expert": me - 4}
    across_y, across_x = {"expert": me + 2 - 4 * y}, {"expert": me + 1 - 2 * x}
    sibling = {"dp": 1 - core}
    second = (across_y, across_x)
    third = (across_x, across_y)
    feats = (xa, xb)
    quarter = half // 2
    left_cols, right_cols = pl.ds(0, quarter), pl.ds(quarter, quarter)
    left = (pl.ds(0, TAG + quarter), left_cols)
    right = (pl.ds(TAG + quarter, quarter), right_cols)

    def when(cond, fn):
        pl.when(cond)(fn)

    def piece(zz):
        if isinstance(zz, int):
            return pl.ds(zz * tok, tok)
        return pl.ds(pl.multiple_of(zz * tok, tok), tok)

    def remote(src, dst, send, recv, device):
        return pltpu.make_async_remote_copy(
            src_ref=src, dst_ref=dst, send_sem=send, recv_sem=recv,
            device_id=device, device_id_type=MESH,
        )

    barrier = pltpu.get_barrier_semaphore()
    for device in (across_y, across_x, sibling):
        pl.semaphore_signal(barrier, inc=1, device_id=device, device_id_type=MESH)

    @pl.when(z < DEPTH - 1)
    def _():
        pl.semaphore_signal(barrier, inc=1, device_id=above, device_id_type=MESH)

    @pl.when(z > 0)
    def _():
        pl.semaphore_signal(barrier, inc=1, device_id=below, device_id_type=MESH)

    xa[0, piece(z), :TAG] = tags_ref[...]
    xa[0, piece(z), TAG:] = rows_ref[:, :half]
    xb[0, piece(z), :] = rows_ref[:, half:]

    edge = jnp.logical_or(z == 0, z == DEPTH - 1)

    @pl.when(edge)
    def _():
        pl.semaphore_wait(barrier, 4)

    @pl.when(jnp.logical_not(edge))
    def _():
        pl.semaphore_wait(barrier, 5)

    def gather(f, src_kind, dst_kind, zz, slot, device):
        return remote(
            feats[f].at[src_kind, piece(zz)], feats[f].at[dst_kind, piece(zz)],
            gather_send.at[f, slot + zz], gather_recv.at[f, dst_kind * DEPTH + zz], device,
        )

    def climb(f, zz):
        return gather(f, 0, 0, zz, 0, above)

    def sink(f, zz):
        return gather(f, 0, 0, zz, 4, below)

    def own_second(f, zz):
        return gather(f, 0, 1, zz, 8, second[f])

    def own_third(f, zz):
        return gather(f, 0, 2, zz, 12, third[f])

    def second_third(f, zz):
        return remote(
            feats[f].at[1, piece(zz), left[f]], feats[f].at[3, piece(zz), left[f]],
            gather_send.at[f, 16 + zz], gather_recv.at[f, 12 + zz], third[f],
        )

    def right_third(f):
        return remote(
            feats[f].at[1, piece(z), right[f]], feats[f].at[3, piece(z), right[f]],
            gather_send.at[f, 28], gather_recv.at[f, 16 + z], third[f],
        )

    def right_line(f, zz, slot, device):
        ref = feats[f].at[3, piece(zz), right[f]]
        return remote(
            ref, ref, gather_send.at[f, slot + zz], gather_recv.at[f, 16 + zz], device
        )

    def right_climb(f, zz):
        return right_line(f, zz, 20, above)

    def right_sink(f, zz):
        return right_line(f, zz, 24, below)

    for f in range(2):
        when(z < DEPTH - 1, lambda f=f: climb(f, z).start())
        when(z > 0, lambda f=f: sink(f, z).start())
        own_second(f, z).start()
    for f in range(2):
        own_third(f, z).start()

    pairs = (
        (gate_ref, w_in.at[:, pl.ds(0, unit)], w_in.at[:, pl.ds(unit, unit)]),
        (up_ref, w_in.at[:, pl.ds(2 * unit, unit)], w_in.at[:, pl.ds(3 * unit, unit)]),
        (down_ref, w_out.at[pl.ds(0, unit)], w_out.at[pl.ds(unit, unit)]),
    )
    swaps = []
    for i, (src, mine, other) in enumerate(pairs):
        local = pltpu.make_async_copy(src, mine, weight_sem.at[3 * i])
        swap = remote(src, other, weight_sem.at[3 * i + 1], weight_sem.at[3 * i + 2], sibling)
        local.start()
        swap.start()
        swaps.append((local, swap))

    def relay_second(zz):
        for f in range(2):
            own_second(f, zz).wait_recv()
            second_third(f, zz).start()

    def send_third(zz):
        for f in range(2):
            own_third(f, zz).start()

    def at_stage(k, fn):
        if k == 0:
            fn(z)
        else:
            when(z >= k, lambda: fn(z - k))
            when(z + k < DEPTH, lambda: fn(z + k))

    def relay_right(k):
        def from_below():
            for f in range(2):
                right_climb(f, z - k).wait_recv()
                when(z < DEPTH - 1, lambda f=f: right_climb(f, z - k).start())

        def from_above():
            for f in range(2):
                right_sink(f, z + k).wait_recv()
                when(z > 0, lambda f=f: right_sink(f, z + k).start())

        when(z >= k, from_below)
        when(z + k < DEPTH, from_above)

    for k in range(1, DEPTH):
        def from_below(k=k):
            zz = z - k
            for f in range(2):
                climb(f, zz).wait_recv()
                when(z < DEPTH - 1, lambda f=f: climb(f, zz).start())
                own_second(f, zz).start()

        def from_above(k=k):
            zz = z + k
            for f in range(2):
                sink(f, zz).wait_recv()
                when(z > 0, lambda f=f: sink(f, zz).start())
                own_second(f, zz).start()

        when(z >= k, from_below)
        when(z + k < DEPTH, from_above)
        at_stage(k - 1, relay_second)
        if k == 1:
            for f in range(2):
                right_third(f).start()
        if k == 2:
            for f in range(2):
                right_third(f).wait_recv()
                when(z < DEPTH - 1, lambda f=f: right_climb(f, z).start())
                when(z > 0, lambda f=f: right_sink(f, z).start())
            at_stage(1, send_third)
        if k == 3:
            relay_right(1)

    def expert(kind_a, kind_b, targets):
        lane = lax.broadcasted_iota(jnp.int32, (DEPTH * tok, TAG), 1)
        mine = jnp.logical_or(lane == me, lane == me + 16)
        tags = xa[kind_a, :, :TAG].astype(jnp.float32)
        weight = jnp.sum(jnp.where(mine, tags, 0.0), axis=1, keepdims=True)

        def hidden_tile(j, carry):
            cols = pl.multiple_of(j * 256, 256)
            gate_cols, up_cols = pl.ds(cols, 256), pl.ds(2 * unit + cols, 256)

            def project(columns):
                return jnp.dot(
                    xa[kind_a, :, TAG:], w_in[:half, columns], preferred_element_type=jnp.float32
                ) + jnp.dot(
                    xb[kind_b], w_in[half:, columns], preferred_element_type=jnp.float32
                )

            gate_act = project(gate_cols)
            up_act = project(up_cols)
            act = gate_act / (1.0 + jnp.exp(-gate_act)) * up_act
            hidden[:, gate_cols] = act.astype(jnp.bfloat16)
            return carry

        lax.fori_loop(0, 2 * unit // 256, hidden_tile, 0)
        for f in range(2):
            target = targets[f]

            def out_tile(j, carry, f=f, target=target):
                cols = pl.multiple_of(j * 512, 512)
                val = jnp.dot(
                    hidden[...], w_out[:, pl.ds(f * half + cols, 512)],
                    preferred_element_type=jnp.float32,
                )
                target[:, pl.ds(cols, 512)] = (val * weight).astype(target.dtype)
                return carry

            lax.fori_loop(0, half // 512, out_tile, 0)

    order = (3, 0, 2, 1)

    def leave_third(f, zz):
        return remote(
            leave.at[f, 0, piece(zz)], got_third.at[f, 0, piece(zz)],
            reduce_send.at[f, zz], reduce_recv.at[f, zz], third[f],
        )

    def leave_both(f, zz):
        return remote(
            leave.at[f, 1, piece(zz), left_cols], got_third.at[f, 1, piece(zz), left_cols],
            reduce_send.at[f, 4 + zz], reduce_recv.at[f, 4 + zz], third[f],
        )

    def leave_right(f):
        return remote(
            leave.at[f, 1, piece(z), right_cols], got_third.at[f, 1, piece(z), right_cols],
            reduce_send.at[f, 28], reduce_recv.at[f, 28], third[f],
        )

    def early_rising(f, zz):
        ref = early_rise.at[f, piece(zz)]
        return remote(ref, ref, reduce_send.at[f, 20 + zz], reduce_recv.at[f, 20 + zz], above)

    def early_falling(f, zz):
        ref = early_fall.at[f, piece(zz)]
        return remote(ref, ref, reduce_send.at[f, 24 + zz], reduce_recv.at[f, 24 + zz], below)

    def leave_second(f, zz):
        return remote(
            got_third.at[f, 1, piece(zz)], got_second.at[f, piece(zz)],
            reduce_send.at[f, 8 + zz], reduce_recv.at[f, 8 + zz], second[f],
        )

    def rising(f, zz):
        return remote(
            rise.at[f, piece(zz)], rise.at[f, piece(zz)],
            reduce_send.at[f, 12 + zz], reduce_recv.at[f, 12 + zz], above,
        )

    def falling(f, zz):
        return remote(
            fall.at[f, piece(zz)], fall.at[f, piece(zz)],
            reduce_send.at[f, 16 + zz], reduce_recv.at[f, 16 + zz], below,
        )

    for local, swap in swaps:
        local.wait()
        swap.wait_recv()
    expert(0, 0, (stay.at[0], stay.at[1]))
    relay_right(2)
    at_stage(3, relay_second)
    at_stage(2, send_third)
    at_stage(3, send_third)

    def wide(ref):
        return ref.astype(jnp.float32)

    def to_second(f, zz):
        def go():
            leave_both(f, zz).wait_recv()
            val = pass_on[f, piece(zz), left_cols] + wide(got_third[f, 1, piece(zz), left_cols])
            got_third[f, 1, piece(zz), left_cols] = val.astype(jnp.bfloat16)
            got_third[f, 1, piece(zz), right_cols] = pass_on[f, piece(zz), right_cols].astype(
                jnp.bfloat16
            )
            leave_second(f, zz).start()

        when(zz != z, go)

    def own_to_second(f):
        leave_both(f, z).wait_recv()
        leave_right(f).wait_recv()
        val = pass_on[f, piece(z), :] + wide(got_third[f, 1, piece(z), :])
        got_third[f, 1, piece(z), :] = val.astype(jnp.bfloat16)
        leave_second(f, z).start()

    def early_relay(buf, copy, zz):
        for f in range(2):
            copy(f, zz).wait_recv()
            val = wide(leave[f, 1, piece(zz), right_cols]) + wide(buf[f, piece(zz), :])
            buf[f, piece(zz), :] = val.astype(jnp.bfloat16)
            copy(f, zz).start()

    def early_up(zz):
        early_relay(early_rise, early_rising, zz)

    def early_down(zz):
        early_relay(early_fall, early_falling, zz)

    def early_first(buf, copy, pieces):
        for zz in pieces:
            for f in range(2):
                buf[f, piece(zz), :] = leave[f, 1, piece(zz), right_cols]
                copy(f, zz).start()

    def early_finish(up, down):
        for f in range(2):
            val = wide(leave[f, 1, piece(z), right_cols])
            if up:
                early_rising(f, z).wait_recv()
                val = val + wide(early_rise[f, piece(z), :])
            if down:
                early_falling(f, z).wait_recv()
                val = val + wide(early_fall[f, piece(z), :])
            leave[f, 1, piece(z), right_cols] = val.astype(jnp.bfloat16)
            leave_right(f).start()

    for zz in range(DEPTH):
        for f in range(2):
            second_third(f, zz).wait_recv()
    relay_right(3)
    expert(3, 3, (leave.at[0, 1], leave.at[1, 1]))
    for zz in order:
        for f in range(2):
            leave_both(f, zz).start()
    when(z == 0, lambda: early_first(early_rise, early_rising, (3, 2, 1)))
    when(z == DEPTH - 1, lambda: early_first(early_fall, early_falling, (0, 1, 2)))

    for zz in range(DEPTH):
        own_third(0, zz).wait_recv()
    expert(2, 1, (leave.at[0, 0], pass_on.at[1]))
    when(z == 1, lambda: early_up(3))
    when(z == 2, lambda: early_down(0))
    for zz in order[:2]:
        to_second(1, zz)
    for zz in order:
        leave_third(0, zz).start()
    for zz in range(DEPTH):
        own_third(1, zz).wait_recv()
    expert(1, 2, (pass_on.at[0], leave.at[1, 0]))
    when(z == 1, lambda: early_down(0))
    when(z == 2, lambda: early_up(3))
    for zz in order[:2]:
        to_second(0, zz)
    for zz in order:
        leave_third(1, zz).start()
    when(z == 1, lambda: early_up(2))
    when(z == 2, lambda: early_down(1))
    for zz in order[2:]:
        for f in range(2):
            to_second(f, zz)
    when(z == 0, lambda: early_finish(False, True))
    when(z == DEPTH - 1, lambda: early_finish(True, False))
    when(jnp.logical_not(edge), lambda: early_finish(True, True))

    def settle(zz):
        for f in range(2):
            leave_third(f, zz).wait_recv()
            leave_second(f, zz).wait_recv()
            stay[f, piece(zz), :] = (
                stay[f, piece(zz), :]
                + wide(got_third[f, 0, piece(zz), :])
                + wide(got_second[f, piece(zz), :])
            )

        def first_up():
            for f in range(2):
                rise[f, piece(zz), :] = stay[f, piece(zz), :].astype(jnp.bfloat16)
                rising(f, zz).start()

        def first_down():
            for f in range(2):
                fall[f, piece(zz), :] = stay[f, piece(zz), :].astype(jnp.bfloat16)
                falling(f, zz).start()

        if not isinstance(zz, int):
            return
        if zz > 0:
            when(z == 0, first_up)
        if zz < DEPTH - 1:
            when(z == DEPTH - 1, first_down)

    def relay_up(zz):
        for f in range(2):
            rising(f, zz).wait_recv()
            val = stay[f, piece(zz), :] + wide(rise[f, piece(zz), :])
            rise[f, piece(zz), :] = val.astype(jnp.bfloat16)
            rising(f, zz).start()

    def relay_down(zz):
        for f in range(2):
            falling(f, zz).wait_recv()
            val = stay[f, piece(zz), :] + wide(fall[f, piece(zz), :])
            fall[f, piece(zz), :] = val.astype(jnp.bfloat16)
            falling(f, zz).start()

    for i in range(1, DEPTH + 1):
        when(z != order[i - 1], lambda i=i: settle(order[i - 1]))
        if i == 2:
            for f in range(2):
                own_to_second(f)
            when(z == 1, lambda: relay_up(3))
            when(z == 2, lambda: relay_down(0))
        if i == 3:
            when(z == 1, lambda: relay_down(0))
            when(z == 2, lambda: relay_up(3))
    when(z == 1, lambda: relay_up(2))
    when(z == 2, lambda: relay_down(1))

    settle(z)
    cols = (pl.ds(0, half), pl.ds(half, half))

    def finish(up, down):
        for f in range(2):
            val = stay[f, piece(z), :]
            if up:
                rising(f, z).wait_recv()
                val = val + wide(rise[f, piece(z), :])
            if down:
                falling(f, z).wait_recv()
                val = val + wide(fall[f, piece(z), :])
            out_ref[:, cols[f]] = val.astype(out_ref.dtype)

    when(z == 0, lambda: finish(False, True))
    when(z == DEPTH - 1, lambda: finish(True, False))
    when(jnp.logical_not(edge), lambda: finish(True, True))

    for _, swap in swaps:
        swap.wait_send()
    for f in range(2):
        for zz in range(DEPTH):
            when(jnp.logical_and(z < DEPTH - 1, zz <= z), lambda f=f, zz=zz: climb(f, zz).wait_send())
            when(jnp.logical_and(z > 0, zz >= z), lambda f=f, zz=zz: sink(f, zz).wait_send())
            for copy in (own_second, own_third, second_third, leave_third, leave_both, leave_second):
                copy(f, zz).wait_send()
            when(zz > z, lambda f=f, zz=zz: rising(f, zz).wait_send())
            when(zz < z, lambda f=f, zz=zz: falling(f, zz).wait_send())
            when(zz > z, lambda f=f, zz=zz: early_rising(f, zz).wait_send())
            when(zz < z, lambda f=f, zz=zz: early_falling(f, zz).wait_send())
            when(jnp.logical_and(z < DEPTH - 1, zz <= z), lambda f=f, zz=zz: right_climb(f, zz).wait_send())
            when(jnp.logical_and(z > 0, zz >= z), lambda f=f, zz=zz: right_sink(f, zz).wait_send())
        right_third(f).wait_send()
        leave_right(f).wait_send()


def fused_body(tokens, routes, gate_probs, gate_w, up_w, down_w):
    experts = lax.axis_size("expert")
    tok, width = tokens.shape
    unit = gate_w.shape[2]
    half = width // 2
    line = DEPTH * tok
    expert_ids = jnp.arange(experts, dtype=jnp.int32)
    named = routes[:, :, None] == expert_ids
    spread = jnp.sum(jnp.where(named, gate_probs[:, :, None], 0.0), axis=1)
    coarse = lax.reduce_precision(spread, 8, 7)
    fine = spread - coarse
    tags = jnp.concatenate([coarse, fine], axis=1).astype(jnp.bfloat16)
    tags = jnp.pad(tags, ((0, 0), (0, TAG - 2 * experts)))
    vmem, anywhere = pl.BlockSpec(memory_space=pltpu.VMEM), pl.BlockSpec(memory_space=pl.ANY)
    bf16, f32, dma = jnp.bfloat16, jnp.float32, pltpu.SemaphoreType.DMA
    return pl.pallas_call(
        fused_kernel,
        out_shape=jax.ShapeDtypeStruct((tok, width), bf16),
        in_specs=[vmem, vmem, anywhere, anywhere, anywhere],
        out_specs=vmem,
        scratch_shapes=[
            pltpu.VMEM((4, line, TAG + half), bf16),
            pltpu.VMEM((4, line, half), bf16),
            pltpu.VMEM((width, 4 * unit), bf16),
            pltpu.VMEM((2 * unit, width), bf16),
            pltpu.VMEM((line, 2 * unit), bf16),
            pltpu.VMEM((2, line, half), f32),
            pltpu.VMEM((2, line, half), f32),
            pltpu.VMEM((2, 2, line, half), bf16),
            pltpu.VMEM((2, 2, line, half), bf16),
            pltpu.VMEM((2, line, half), bf16),
            pltpu.VMEM((2, line, half), bf16),
            pltpu.VMEM((2, line, half), bf16),
            pltpu.VMEM((2, line, half // 2), bf16),
            pltpu.VMEM((2, line, half // 2), bf16),
            dma((2, 29)),
            dma((2, 20)),
            dma((2, 29)),
            dma((2, 29)),
            dma((9,)),
        ],
        compiler_params=pltpu.CompilerParams(
            collective_id=0, has_side_effects=True, vmem_limit_bytes=60 * 2**20
        ),
        cost_estimate=pl.CostEstimate(
            flops=2 * experts * tok * width * unit * 6,
            bytes_accessed=6 * width * unit * 2,
            transcendentals=experts * tok * unit * 2,
        ),
    )(tokens, tags, gate_w[0], up_w[0], down_w[0])


def body(tokens, routes, *others):
    tok_count, top_count = routes.shape
    experts = lax.axis_size("expert")
    capacity = 2 * tok_count * top_count // experts
    if capacity >= tok_count and experts == 4 * DEPTH and lax.axis_size("dp") == 2:
        return fused_body(tokens, routes, *others)
    return exchange_body(tokens, routes, *others)


def solution(mesh):
    return jax.shard_map(
        body,
        mesh=mesh,
        in_specs=(
            P(("expert", "dp"), None),
            P(("expert", "dp"), None),
            P(("expert", "dp"), None),
            P("expert", None, "dp"),
            P("expert", None, "dp"),
            P("expert", "dp", None),
        ),
        out_specs=P(("expert", "dp"), None),
        check_vma=False,
    )
```

```python
import jax
import jax.numpy as jnp
from jax import lax
from jax.experimental import pallas as pl
from jax.experimental.pallas import tpu as pltpu
from jax.sharding import PartitionSpec as P


def swiglu(row_block, w_gate, w_up, w_down):
    gate_act = jnp.dot(row_block, w_gate, preferred_element_type=jnp.float32)
    up_act = jnp.dot(row_block, w_up, preferred_element_type=jnp.float32)
    hidden = (jax.nn.silu(gate_act) * up_act).astype(jnp.bfloat16)
    return jnp.dot(hidden, w_down, preferred_element_type=jnp.float32)


def apply_expert(row_block, w_gate, w_up, w_down):
    return swiglu(row_block, w_gate, w_up, w_down)


def exchange_body(tokens, routes, gate_probs, gate_w, up_w, down_w):
    experts = lax.axis_size("expert")
    tok_count, model_width = tokens.shape
    top_count = routes.shape[1]
    capacity = 2 * tok_count * top_count // experts
    expert_ids = jnp.arange(experts, dtype=jnp.int32)
    named_hits = jnp.sum((routes[:, :, None] == expert_ids).astype(jnp.int32), axis=1)
    before = jnp.cumsum(named_hits, axis=0) - named_hits
    slot_index = jnp.take_along_axis(before, routes, axis=1)
    target = routes * capacity + slot_index
    buffer_rows = jnp.arange(experts * capacity, dtype=jnp.int32)
    placer = jnp.sum(
        (target[None, :, :] == buffer_rows[:, None, None]).astype(jnp.float32), axis=2
    ).astype(jnp.bfloat16)
    outgoing = jnp.dot(placer, tokens, preferred_element_type=jnp.float32).astype(jnp.bfloat16)
    outgoing = outgoing.reshape(experts, capacity, model_width)
    present = (
        jnp.sum(placer.astype(jnp.float32), axis=1).astype(jnp.bfloat16).reshape(experts, capacity)
    )
    w_gate = gate_w[0]
    w_up = up_w[0]
    w_down = down_w[0]
    row_block = lax.all_to_all(outgoing, "expert", split_axis=0, concat_axis=0, tiled=True)
    flag_block = lax.all_to_all(present, "expert", split_axis=0, concat_axis=0, tiled=True)
    source_count = row_block.shape[0]
    item_count = row_block.shape[1]
    flat_rows = row_block.reshape(-1, model_width)
    flat_flags = flag_block.reshape(-1)
    both_rows = lax.all_gather(flat_rows, "dp", axis=0, tiled=True)
    partial_out = apply_expert(both_rows, w_gate, w_up, w_down)
    result = lax.psum_scatter(partial_out, "dp", scatter_dimension=0, tiled=True)
    masked = result * flat_flags.astype(jnp.float32)[:, None]
    answered = masked.astype(jnp.bfloat16).reshape(source_count, item_count, model_width)
    returned = lax.all_to_all(answered, "expert", split_axis=0, concat_axis=0, tiled=True)
    picked = returned.reshape(experts * capacity, model_width)[target]
    mixed_out = jnp.einsum(
        "tk,tkd->td", gate_probs, picked.astype(jnp.float32), precision=lax.Precision.HIGHEST
    )
    return mixed_out.astype(jnp.bfloat16)


MESH = pl.DeviceIdType.MESH
DEPTH = 4
TAG = 128


def fused_kernel(
    rows_ref, tags_ref, gate_ref, up_ref, down_ref, out_ref,
    xa, xb, w_in, w_out, hidden, stay, pass_on, leave, got_third, got_second, rise, fall, early_rise, early_fall,
    gather_send, gather_recv, reduce_send, reduce_recv, weight_sem,
):
    tok = rows_ref.shape[0]
    half = xb.shape[2]
    unit = gate_ref.shape[1]
    me = lax.axis_index("expert")
    core = lax.axis_index("dp")
    z = me // 4
    y = (me // 2) % 2
    x = me % 2
    above, below = {"expert": me + 4}, {"expert": me - 4}
    across_y, across_x = {"expert": me + 2 - 4 * y}, {"expert": me + 1 - 2 * x}
    sibling = {"dp": 1 - core}
    second = (across_y, across_x)
    third = (across_x, across_y)
    feats = (xa, xb)
    quarter = half // 2
    left_cols, right_cols = pl.ds(0, quarter), pl.ds(quarter, quarter)
    left = (pl.ds(0, TAG + quarter), left_cols)
    right = (pl.ds(TAG + quarter, quarter), right_cols)

    def when(cond, fn):
        pl.when(cond)(fn)

    def piece(zz):
        if isinstance(zz, int):
            return pl.ds(zz * tok, tok)
        return pl.ds(pl.multiple_of(zz * tok, tok), tok)

    def remote(src, dst, send, recv, device):
        return pltpu.make_async_remote_copy(
            src_ref=src, dst_ref=dst, send_sem=send, recv_sem=recv,
            device_id=device, device_id_type=MESH,
        )

    barrier = pltpu.get_barrier_semaphore()
    for device in (across_y, across_x, sibling):
        pl.semaphore_signal(barrier, inc=1, device_id=device, device_id_type=MESH)

    @pl.when(z < DEPTH - 1)
    def _():
        pl.semaphore_signal(barrier, inc=1, device_id=above, device_id_type=MESH)

    @pl.when(z > 0)
    def _():
        pl.semaphore_signal(barrier, inc=1, device_id=below, device_id_type=MESH)

    xa[0, piece(z), :TAG] = tags_ref[...]
    xa[0, piece(z), TAG:] = rows_ref[:, :half]
    xb[0, piece(z), :] = rows_ref[:, half:]

    edge = jnp.logical_or(z == 0, z == DEPTH - 1)

    @pl.when(edge)
    def _():
        pl.semaphore_wait(barrier, 4)

    @pl.when(jnp.logical_not(edge))
    def _():
        pl.semaphore_wait(barrier, 5)

    def gather(f, src_kind, dst_kind, zz, slot, device):
        return remote(
            feats[f].at[src_kind, piece(zz)], feats[f].at[dst_kind, piece(zz)],
            gather_send.at[f, slot + zz], gather_recv.at[f, dst_kind * DEPTH + zz], device,
        )

    def climb(f, zz):
        return gather(f, 0, 0, zz, 0, above)

    def sink(f, zz):
        return gather(f, 0, 0, zz, 4, below)

    def own_second(f, zz):
        return gather(f, 0, 1, zz, 8, second[f])

    def own_third(f, zz):
        return gather(f, 0, 2, zz, 12, third[f])

    def second_third(f, zz):
        return remote(
            feats[f].at[1, piece(zz), left[f]], feats[f].at[3, piece(zz), left[f]],
            gather_send.at[f, 16 + zz], gather_recv.at[f, 12 + zz], third[f],
        )

    def right_third(f):
        return remote(
            feats[f].at[1, piece(z), right[f]], feats[f].at[3, piece(z), right[f]],
            gather_send.at[f, 28], gather_recv.at[f, 16 + z], third[f],
        )

    def right_line(f, zz, slot, device):
        ref = feats[f].at[3, piece(zz), right[f]]
        return remote(
            ref, ref, gather_send.at[f, slot + zz], gather_recv.at[f, 16 + zz], device
        )

    def right_climb(f, zz):
        return right_line(f, zz, 20, above)

    def right_sink(f, zz):
        return right_line(f, zz, 24, below)

    for f in range(2):
        when(z < DEPTH - 1, lambda f=f: climb(f, z).start())
        when(z > 0, lambda f=f: sink(f, z).start())
        own_second(f, z).start()
    for f in range(2):
        own_third(f, z).start()

    pairs = (
        (gate_ref, w_in.at[:, pl.ds(0, unit)], w_in.at[:, pl.ds(unit, unit)]),
        (up_ref, w_in.at[:, pl.ds(2 * unit, unit)], w_in.at[:, pl.ds(3 * unit, unit)]),
        (down_ref, w_out.at[pl.ds(0, unit)], w_out.at[pl.ds(unit, unit)]),
    )
    swaps = []
    for i, (src, mine, other) in enumerate(pairs):
        local = pltpu.make_async_copy(src, mine, weight_sem.at[3 * i])
        swap = remote(src, other, weight_sem.at[3 * i + 1], weight_sem.at[3 * i + 2], sibling)
        local.start()
        swap.start()
        swaps.append((local, swap))

    def relay_second(zz):
        for f in range(2):
            own_second(f, zz).wait_recv()
            second_third(f, zz).start()

    def send_third(zz):
        own_third(0, zz).start()

    def at_stage(k, fn):
        if k == 0:
            fn(z)
        else:
            when(z >= k, lambda: fn(z - k))
            when(z + k < DEPTH, lambda: fn(z + k))

    def relay_right(k):
        def from_below():
            for f in range(2):
                right_climb(f, z - k).wait_recv()
                when(z < DEPTH - 1, lambda f=f: right_climb(f, z - k).start())

        def from_above():
            for f in range(2):
                right_sink(f, z + k).wait_recv()
                when(z > 0, lambda f=f: right_sink(f, z + k).start())

        when(z >= k, from_below)
        when(z + k < DEPTH, from_above)

    for k in range(1, DEPTH):
        def from_below(k=k):
            zz = z - k
            for f in range(2):
                climb(f, zz).wait_recv()
                when(z < DEPTH - 1, lambda f=f: climb(f, zz).start())
                own_second(f, zz).start()
            own_third(1, zz).start()

        def from_above(k=k):
            zz = z + k
            for f in range(2):
                sink(f, zz).wait_recv()
                when(z > 0, lambda f=f: sink(f, zz).start())
                own_second(f, zz).start()
            own_third(1, zz).start()

        when(z >= k, from_below)
        when(z + k < DEPTH, from_above)
        at_stage(k - 1, relay_second)
        if k == 1:
            for f in range(2):
                right_third(f).start()
        if k == 2:
            for f in range(2):
                right_third(f).wait_recv()
                when(z < DEPTH - 1, lambda f=f: right_climb(f, z).start())
                when(z > 0, lambda f=f: right_sink(f, z).start())
            at_stage(1, send_third)
        if k == 3:
            relay_right(1)

    def expert(kind_a, kind_b, targets):
        lane = lax.broadcasted_iota(jnp.int32, (DEPTH * tok, TAG), 1)
        mine = jnp.logical_or(lane == me, lane == me + 16)
        tags = xa[kind_a, :, :TAG].astype(jnp.float32)
        weight = jnp.sum(jnp.where(mine, tags, 0.0), axis=1, keepdims=True)

        def hidden_tile(j, carry):
            cols = pl.multiple_of(j * 256, 256)
            gate_cols, up_cols = pl.ds(cols, 256), pl.ds(2 * unit + cols, 256)

            def project(columns):
                return jnp.dot(
                    xa[kind_a, :, TAG:], w_in[:half, columns], preferred_element_type=jnp.float32
                ) + jnp.dot(
                    xb[kind_b], w_in[half:, columns], preferred_element_type=jnp.float32
                )

            gate_act = project(gate_cols)
            up_act = project(up_cols)
            act = gate_act / (1.0 + jnp.exp(-gate_act)) * up_act
            hidden[:, gate_cols] = act.astype(jnp.bfloat16)
            return carry

        lax.fori_loop(0, 2 * unit // 256, hidden_tile, 0)
        for f in range(2):
            target = targets[f]

            def out_tile(j, carry, f=f, target=target):
                cols = pl.multiple_of(j * 512, 512)
                val = jnp.dot(
                    hidden[...], w_out[:, pl.ds(f * half + cols, 512)],
                    preferred_element_type=jnp.float32,
                )
                target[:, pl.ds(cols, 512)] = (val * weight).astype(target.dtype)
                return carry

            lax.fori_loop(0, half // 512, out_tile, 0)

    order = (3, 0, 2, 1)

    def leave_third(f, zz):
        return remote(
            leave.at[f, 0, piece(zz)], got_third.at[f, 0, piece(zz)],
            reduce_send.at[f, zz], reduce_recv.at[f, zz], third[f],
        )

    def leave_both(f, zz):
        return remote(
            leave.at[f, 1, piece(zz), left_cols], got_third.at[f, 1, piece(zz), left_cols],
            reduce_send.at[f, 4 + zz], reduce_recv.at[f, 4 + zz], third[f],
        )

    def leave_right(f):
        return remote(
            leave.at[f, 1, piece(z), right_cols], got_third.at[f, 1, piece(z), right_cols],
            reduce_send.at[f, 28], reduce_recv.at[f, 28], third[f],
        )

    def early_rising(f, zz):
        ref = early_rise.at[f, piece(zz)]
        return remote(ref, ref, reduce_send.at[f, 20 + zz], reduce_recv.at[f, 20 + zz], above)

    def early_falling(f, zz):
        ref = early_fall.at[f, piece(zz)]
        return remote(ref, ref, reduce_send.at[f, 24 + zz], reduce_recv.at[f, 24 + zz], below)

    def leave_second(f, zz):
        return remote(
            got_third.at[f, 1, piece(zz)], got_second.at[f, piece(zz)],
            reduce_send.at[f, 8 + zz], reduce_recv.at[f, 8 + zz], second[f],
        )

    def rising(f, zz):
        return remote(
            rise.at[f, piece(zz)], rise.at[f, piece(zz)],
            reduce_send.at[f, 12 + zz], reduce_recv.at[f, 12 + zz], above,
        )

    def falling(f, zz):
        return remote(
            fall.at[f, piece(zz)], fall.at[f, piece(zz)],
            reduce_send.at[f, 16 + zz], reduce_recv.at[f, 16 + zz], below,
        )

    for local, swap in swaps:
        local.wait()
        swap.wait_recv()
    expert(0, 0, (stay.at[0], stay.at[1]))
    relay_right(2)
    at_stage(3, relay_second)
    at_stage(2, send_third)
    at_stage(3, send_third)

    def wide(ref):
        return ref.astype(jnp.float32)

    def to_second(f, zz):
        def go():
            leave_both(f, zz).wait_recv()
            val = pass_on[f, piece(zz), left_cols] + wide(got_third[f, 1, piece(zz), left_cols])
            got_third[f, 1, piece(zz), left_cols] = val.astype(jnp.bfloat16)
            got_third[f, 1, piece(zz), right_cols] = pass_on[f, piece(zz), right_cols].astype(
                jnp.bfloat16
            )
            leave_second(f, zz).start()

        when(zz != z, go)

    def own_to_second(f):
        leave_both(f, z).wait_recv()
        leave_right(f).wait_recv()
        val = pass_on[f, piece(z), :] + wide(got_third[f, 1, piece(z), :])
        got_third[f, 1, piece(z), :] = val.astype(jnp.bfloat16)
        leave_second(f, z).start()

    def early_relay(buf, copy, zz):
        for f in range(2):
            copy(f, zz).wait_recv()
            val = wide(leave[f, 1, piece(zz), right_cols]) + wide(buf[f, piece(zz), :])
            buf[f, piece(zz), :] = val.astype(jnp.bfloat16)
            copy(f, zz).start()

    def early_up(zz):
        early_relay(early_rise, early_rising, zz)

    def early_down(zz):
        early_relay(early_fall, early_falling, zz)

    def early_first(buf, copy, pieces):
        for zz in pieces:
            for f in range(2):
                buf[f, piece(zz), :] = leave[f, 1, piece(zz), right_cols]
                copy(f, zz).start()

    def early_finish(up, down):
        for f in range(2):
            val = wide(leave[f, 1, piece(z), right_cols])
            if up:
                early_rising(f, z).wait_recv()
                val = val + wide(early_rise[f, piece(z), :])
            if down:
                early_falling(f, z).wait_recv()
                val = val + wide(early_fall[f, piece(z), :])
            leave[f, 1, piece(z), right_cols] = val.astype(jnp.bfloat16)
            leave_right(f).start()

    for zz in range(DEPTH):
        own_third(1, zz).wait_recv()
    expert(1, 2, (pass_on.at[0], leave.at[1, 0]))
    for zz in order[:2]:
        leave_third(1, zz).start()
    for zz in range(DEPTH):
        for f in range(2):
            second_third(f, zz).wait_recv()
    relay_right(3)
    expert(3, 3, (leave.at[0, 1], leave.at[1, 1]))
    for zz in order:
        for f in range(2):
            leave_both(f, zz).start()
    when(z == 0, lambda: early_first(early_rise, early_rising, (3, 2, 1)))
    when(z == DEPTH - 1, lambda: early_first(early_fall, early_falling, (0, 1, 2)))
    for zz in order[2:]:
        leave_third(1, zz).start()

    for zz in range(DEPTH):
        own_third(0, zz).wait_recv()
    expert(2, 1, (leave.at[0, 0], pass_on.at[1]))
    for zz in order[:2]:
        leave_third(0, zz).start()
    when(z == 1, lambda: early_up(3))
    when(z == 2, lambda: early_down(0))
    for zz in order[:2]:
        for f in range(2):
            to_second(f, zz)
    for zz in order[2:]:
        leave_third(0, zz).start()
    when(z == 1, lambda: early_down(0))
    when(z == 2, lambda: early_up(3))
    for zz in order[2:]:
        for f in range(2):
            to_second(f, zz)
    when(z == 1, lambda: early_up(2))
    when(z == 2, lambda: early_down(1))
    when(z == 0, lambda: early_finish(False, True))
    when(z == DEPTH - 1, lambda: early_finish(True, False))
    when(jnp.logical_not(edge), lambda: early_finish(True, True))

    def settle(zz):
        for f in range(2):
            leave_third(f, zz).wait_recv()
            leave_second(f, zz).wait_recv()
            stay[f, piece(zz), :] = (
                stay[f, piece(zz), :]
                + wide(got_third[f, 0, piece(zz), :])
                + wide(got_second[f, piece(zz), :])
            )

        def first_up():
            for f in range(2):
                rise[f, piece(zz), :] = stay[f, piece(zz), :].astype(jnp.bfloat16)
                rising(f, zz).start()

        def first_down():
            for f in range(2):
                fall[f, piece(zz), :] = stay[f, piece(zz), :].astype(jnp.bfloat16)
                falling(f, zz).start()

        if not isinstance(zz, int):
            return
        if zz > 0:
            when(z == 0, first_up)
        if zz < DEPTH - 1:
            when(z == DEPTH - 1, first_down)

    def relay_up(zz):
        for f in range(2):
            rising(f, zz).wait_recv()
            val = stay[f, piece(zz), :] + wide(rise[f, piece(zz), :])
            rise[f, piece(zz), :] = val.astype(jnp.bfloat16)
            rising(f, zz).start()

    def relay_down(zz):
        for f in range(2):
            falling(f, zz).wait_recv()
            val = stay[f, piece(zz), :] + wide(fall[f, piece(zz), :])
            fall[f, piece(zz), :] = val.astype(jnp.bfloat16)
            falling(f, zz).start()

    for i in range(1, DEPTH + 1):
        when(z != order[i - 1], lambda i=i: settle(order[i - 1]))
        if i == 2:
            for f in range(2):
                own_to_second(f)
            when(z == 1, lambda: relay_up(3))
            when(z == 2, lambda: relay_down(0))
        if i == 3:
            when(z == 1, lambda: relay_down(0))
            when(z == 2, lambda: relay_up(3))
    when(z == 1, lambda: relay_up(2))
    when(z == 2, lambda: relay_down(1))

    settle(z)
    cols = (pl.ds(0, half), pl.ds(half, half))

    def finish(up, down):
        for f in range(2):
            val = stay[f, piece(z), :]
            if up:
                rising(f, z).wait_recv()
                val = val + wide(rise[f, piece(z), :])
            if down:
                falling(f, z).wait_recv()
                val = val + wide(fall[f, piece(z), :])
            out_ref[:, cols[f]] = val.astype(out_ref.dtype)

    when(z == 0, lambda: finish(False, True))
    when(z == DEPTH - 1, lambda: finish(True, False))
    when(jnp.logical_not(edge), lambda: finish(True, True))

    for _, swap in swaps:
        swap.wait_send()
    for f in range(2):
        for zz in range(DEPTH):
            when(jnp.logical_and(z < DEPTH - 1, zz <= z), lambda f=f, zz=zz: climb(f, zz).wait_send())
            when(jnp.logical_and(z > 0, zz >= z), lambda f=f, zz=zz: sink(f, zz).wait_send())
            for copy in (own_second, own_third, second_third, leave_third, leave_both, leave_second):
                copy(f, zz).wait_send()
            when(zz > z, lambda f=f, zz=zz: rising(f, zz).wait_send())
            when(zz < z, lambda f=f, zz=zz: falling(f, zz).wait_send())
            when(zz > z, lambda f=f, zz=zz: early_rising(f, zz).wait_send())
            when(zz < z, lambda f=f, zz=zz: early_falling(f, zz).wait_send())
            when(jnp.logical_and(z < DEPTH - 1, zz <= z), lambda f=f, zz=zz: right_climb(f, zz).wait_send())
            when(jnp.logical_and(z > 0, zz >= z), lambda f=f, zz=zz: right_sink(f, zz).wait_send())
        right_third(f).wait_send()
        leave_right(f).wait_send()


def fused_body(tokens, routes, gate_probs, gate_w, up_w, down_w):
    experts = lax.axis_size("expert")
    tok, width = tokens.shape
    unit = gate_w.shape[2]
    half = width // 2
    line = DEPTH * tok
    expert_ids = jnp.arange(experts, dtype=jnp.int32)
    named = routes[:, :, None] == expert_ids
    spread = jnp.sum(jnp.where(named, gate_probs[:, :, None], 0.0), axis=1)
    coarse = lax.reduce_precision(spread, 8, 7)
    fine = spread - coarse
    tags = jnp.concatenate([coarse, fine], axis=1).astype(jnp.bfloat16)
    tags = jnp.pad(tags, ((0, 0), (0, TAG - 2 * experts)))
    vmem, anywhere = pl.BlockSpec(memory_space=pltpu.VMEM), pl.BlockSpec(memory_space=pl.ANY)
    bf16, f32, dma = jnp.bfloat16, jnp.float32, pltpu.SemaphoreType.DMA
    return pl.pallas_call(
        fused_kernel,
        out_shape=jax.ShapeDtypeStruct((tok, width), bf16),
        in_specs=[vmem, vmem, anywhere, anywhere, anywhere],
        out_specs=vmem,
        scratch_shapes=[
            pltpu.VMEM((4, line, TAG + half), bf16),
            pltpu.VMEM((4, line, half), bf16),
            pltpu.VMEM((width, 4 * unit), bf16),
            pltpu.VMEM((2 * unit, width), bf16),
            pltpu.VMEM((line, 2 * unit), bf16),
            pltpu.VMEM((2, line, half), f32),
            pltpu.VMEM((2, line, half), f32),
            pltpu.VMEM((2, 2, line, half), bf16),
            pltpu.VMEM((2, 2, line, half), bf16),
            pltpu.VMEM((2, line, half), bf16),
            pltpu.VMEM((2, line, half), bf16),
            pltpu.VMEM((2, line, half), bf16),
            pltpu.VMEM((2, line, half // 2), bf16),
            pltpu.VMEM((2, line, half // 2), bf16),
            dma((2, 29)),
            dma((2, 20)),
            dma((2, 29)),
            dma((2, 29)),
            dma((9,)),
        ],
        compiler_params=pltpu.CompilerParams(
            collective_id=0, has_side_effects=True, vmem_limit_bytes=60 * 2**20
        ),
        cost_estimate=pl.CostEstimate(
            flops=2 * experts * tok * width * unit * 6,
            bytes_accessed=6 * width * unit * 2,
            transcendentals=experts * tok * unit * 2,
        ),
    )(tokens, tags, gate_w[0], up_w[0], down_w[0])


def body(tokens, routes, *others):
    tok_count, top_count = routes.shape
    experts = lax.axis_size("expert")
    capacity = 2 * tok_count * top_count // experts
    if capacity >= tok_count and experts == 4 * DEPTH and lax.axis_size("dp") == 2:
        return fused_body(tokens, routes, *others)
    return exchange_body(tokens, routes, *others)


def solution(mesh):
    return jax.shard_map(
        body,
        mesh=mesh,
        in_specs=(
            P(("expert", "dp"), None),
            P(("expert", "dp"), None),
            P(("expert", "dp"), None),
            P("expert", None, "dp"),
            P("expert", None, "dp"),
            P("expert", "dp", None),
        ),
        out_specs=P(("expert", "dp"), None),
        check_vma=False,
    )
```

```python
import jax
import jax.numpy as jnp
from jax import lax
from jax.experimental import pallas as pl
from jax.experimental.pallas import tpu as pltpu
from jax.sharding import PartitionSpec as P


def swiglu(row_block, w_gate, w_up, w_down):
    gate_act = jnp.dot(row_block, w_gate, preferred_element_type=jnp.float32)
    up_act = jnp.dot(row_block, w_up, preferred_element_type=jnp.float32)
    hidden = (jax.nn.silu(gate_act) * up_act).astype(jnp.bfloat16)
    return jnp.dot(hidden, w_down, preferred_element_type=jnp.float32)


def apply_expert(row_block, w_gate, w_up, w_down):
    return swiglu(row_block, w_gate, w_up, w_down)


def exchange_body(tokens, routes, gate_probs, gate_w, up_w, down_w):
    experts = lax.axis_size("expert")
    tok_count, model_width = tokens.shape
    top_count = routes.shape[1]
    capacity = 2 * tok_count * top_count // experts
    expert_ids = jnp.arange(experts, dtype=jnp.int32)
    named_hits = jnp.sum((routes[:, :, None] == expert_ids).astype(jnp.int32), axis=1)
    before = jnp.cumsum(named_hits, axis=0) - named_hits
    slot_index = jnp.take_along_axis(before, routes, axis=1)
    target = routes * capacity + slot_index
    buffer_rows = jnp.arange(experts * capacity, dtype=jnp.int32)
    placer = jnp.sum(
        (target[None, :, :] == buffer_rows[:, None, None]).astype(jnp.float32), axis=2
    ).astype(jnp.bfloat16)
    outgoing = jnp.dot(placer, tokens, preferred_element_type=jnp.float32).astype(jnp.bfloat16)
    outgoing = outgoing.reshape(experts, capacity, model_width)
    present = (
        jnp.sum(placer.astype(jnp.float32), axis=1).astype(jnp.bfloat16).reshape(experts, capacity)
    )
    w_gate = gate_w[0]
    w_up = up_w[0]
    w_down = down_w[0]
    row_block = lax.all_to_all(outgoing, "expert", split_axis=0, concat_axis=0, tiled=True)
    flag_block = lax.all_to_all(present, "expert", split_axis=0, concat_axis=0, tiled=True)
    source_count = row_block.shape[0]
    item_count = row_block.shape[1]
    flat_rows = row_block.reshape(-1, model_width)
    flat_flags = flag_block.reshape(-1)
    both_rows = lax.all_gather(flat_rows, "dp", axis=0, tiled=True)
    partial_out = apply_expert(both_rows, w_gate, w_up, w_down)
    result = lax.psum_scatter(partial_out, "dp", scatter_dimension=0, tiled=True)
    masked = result * flat_flags.astype(jnp.float32)[:, None]
    answered = masked.astype(jnp.bfloat16).reshape(source_count, item_count, model_width)
    returned = lax.all_to_all(answered, "expert", split_axis=0, concat_axis=0, tiled=True)
    picked = returned.reshape(experts * capacity, model_width)[target]
    mixed_out = jnp.einsum(
        "tk,tkd->td", gate_probs, picked.astype(jnp.float32), precision=lax.Precision.HIGHEST
    )
    return mixed_out.astype(jnp.bfloat16)


MESH = pl.DeviceIdType.MESH
DEPTH = 4
TAG = 128


def fused_kernel(
    rows_ref, tags_ref, gate_ref, up_ref, down_ref, out_ref,
    xa, xb, w_in, w_out, hidden, stay, pass_on, leave, got_third, got_second, rise, fall, early_rise, early_fall,
    gather_send, gather_recv, reduce_send, reduce_recv, weight_sem,
):
    tok = rows_ref.shape[0]
    half = xb.shape[2]
    unit = gate_ref.shape[1]
    me = lax.axis_index("expert")
    core = lax.axis_index("dp")
    z = me // 4
    y = (me // 2) % 2
    x = me % 2
    above, below = {"expert": me + 4}, {"expert": me - 4}
    across_y, across_x = {"expert": me + 2 - 4 * y}, {"expert": me + 1 - 2 * x}
    sibling = {"dp": 1 - core}
    second = (across_y, across_x)
    third = (across_x, across_y)
    feats = (xa, xb)
    quarter = half // 2
    left_cols, right_cols = pl.ds(0, quarter), pl.ds(quarter, quarter)
    left = (pl.ds(0, TAG + quarter), left_cols)
    right = (pl.ds(TAG + quarter, quarter), right_cols)

    def when(cond, fn):
        pl.when(cond)(fn)

    def piece(zz):
        if isinstance(zz, int):
            return pl.ds(zz * tok, tok)
        return pl.ds(pl.multiple_of(zz * tok, tok), tok)

    def remote(src, dst, send, recv, device):
        return pltpu.make_async_remote_copy(
            src_ref=src, dst_ref=dst, send_sem=send, recv_sem=recv,
            device_id=device, device_id_type=MESH,
        )

    barrier = pltpu.get_barrier_semaphore()
    for device in (across_y, across_x, sibling):
        pl.semaphore_signal(barrier, inc=1, device_id=device, device_id_type=MESH)

    @pl.when(z < DEPTH - 1)
    def _():
        pl.semaphore_signal(barrier, inc=1, device_id=above, device_id_type=MESH)

    @pl.when(z > 0)
    def _():
        pl.semaphore_signal(barrier, inc=1, device_id=below, device_id_type=MESH)

    xa[0, piece(z), :TAG] = tags_ref[...]
    xa[0, piece(z), TAG:] = rows_ref[:, :half]
    xb[0, piece(z), :] = rows_ref[:, half:]

    edge = jnp.logical_or(z == 0, z == DEPTH - 1)

    @pl.when(edge)
    def _():
        pl.semaphore_wait(barrier, 4)

    @pl.when(jnp.logical_not(edge))
    def _():
        pl.semaphore_wait(barrier, 5)

    def gather(f, src_kind, dst_kind, zz, slot, device):
        return remote(
            feats[f].at[src_kind, piece(zz)], feats[f].at[dst_kind, piece(zz)],
            gather_send.at[f, slot + zz], gather_recv.at[f, dst_kind * DEPTH + zz], device,
        )

    def climb(f, zz):
        return gather(f, 0, 0, zz, 0, above)

    def sink(f, zz):
        return gather(f, 0, 0, zz, 4, below)

    def own_second(f, zz):
        return gather(f, 0, 1, zz, 8, second[f])

    def own_third(f, zz):
        return gather(f, 0, 2, zz, 12, third[f])

    def second_third(f, zz):
        return remote(
            feats[f].at[1, piece(zz), left[f]], feats[f].at[3, piece(zz), left[f]],
            gather_send.at[f, 16 + zz], gather_recv.at[f, 12 + zz], third[f],
        )

    def right_third(f):
        return remote(
            feats[f].at[1, piece(z), right[f]], feats[f].at[3, piece(z), right[f]],
            gather_send.at[f, 28], gather_recv.at[f, 16 + z], third[f],
        )

    def right_line(f, zz, slot, device):
        ref = feats[f].at[3, piece(zz), right[f]]
        return remote(
            ref, ref, gather_send.at[f, slot + zz], gather_recv.at[f, 16 + zz], device
        )

    def right_climb(f, zz):
        return right_line(f, zz, 20, above)

    def right_sink(f, zz):
        return right_line(f, zz, 24, below)

    for f in range(2):
        when(z < DEPTH - 1, lambda f=f: climb(f, z).start())
        when(z > 0, lambda f=f: sink(f, z).start())
        own_second(f, z).start()
    for f in range(2):
        own_third(f, z).start()

    pairs = (
        (gate_ref, w_in.at[:, pl.ds(0, unit)], w_in.at[:, pl.ds(unit, unit)]),
        (up_ref, w_in.at[:, pl.ds(2 * unit, unit)], w_in.at[:, pl.ds(3 * unit, unit)]),
        (down_ref, w_out.at[pl.ds(0, unit)], w_out.at[pl.ds(unit, unit)]),
    )
    swaps = []
    for i, (src, mine, other) in enumerate(pairs):
        local = pltpu.make_async_copy(src, mine, weight_sem.at[3 * i])
        swap = remote(src, other, weight_sem.at[3 * i + 1], weight_sem.at[3 * i + 2], sibling)
        local.start()
        swap.start()
        swaps.append((local, swap))

    def relay_second(zz):
        for f in range(2):
            own_second(f, zz).wait_recv()
            second_third(f, zz).start()

    def send_third(zz):
        for f in range(2):
            own_third(f, zz).start()

    def at_stage(k, fn):
        if k == 0:
            fn(z)
        else:
            when(z >= k, lambda: fn(z - k))
            when(z + k < DEPTH, lambda: fn(z + k))

    def relay_right(k):
        def from_below():
            for f in range(2):
                right_climb(f, z - k).wait_recv()
                when(z < DEPTH - 1, lambda f=f: right_climb(f, z - k).start())

        def from_above():
            for f in range(2):
                right_sink(f, z + k).wait_recv()
                when(z > 0, lambda f=f: right_sink(f, z + k).start())

        when(z >= k, from_below)
        when(z + k < DEPTH, from_above)

    for k in range(1, DEPTH):
        def from_below(k=k):
            zz = z - k
            for f in range(2):
                climb(f, zz).wait_recv()
                when(z < DEPTH - 1, lambda f=f: climb(f, zz).start())
                own_second(f, zz).start()

        def from_above(k=k):
            zz = z + k
            for f in range(2):
                sink(f, zz).wait_recv()
                when(z > 0, lambda f=f: sink(f, zz).start())
                own_second(f, zz).start()

        when(z >= k, from_below)
        when(z + k < DEPTH, from_above)
        at_stage(k - 1, relay_second)
        if k == 1:
            for f in range(2):
                right_third(f).start()
        if k == 2:
            for f in range(2):
                right_third(f).wait_recv()
                when(z < DEPTH - 1, lambda f=f: right_climb(f, z).start())
                when(z > 0, lambda f=f: right_sink(f, z).start())
            at_stage(1, send_third)
        if k == 3:
            relay_right(1)

    def expert(kind_a, kind_b, targets):
        lane = lax.broadcasted_iota(jnp.int32, (DEPTH * tok, TAG), 1)
        mine = jnp.logical_or(lane == me, lane == me + 16)
        tags = xa[kind_a, :, :TAG].astype(jnp.float32)
        weight = jnp.sum(jnp.where(mine, tags, 0.0), axis=1, keepdims=True)

        def hidden_tile(j, carry):
            cols = pl.multiple_of(j * 256, 256)
            gate_cols, up_cols = pl.ds(cols, 256), pl.ds(2 * unit + cols, 256)

            def project(columns):
                return jnp.dot(
                    xa[kind_a, :, TAG:], w_in[:half, columns], preferred_element_type=jnp.float32
                ) + jnp.dot(
                    xb[kind_b], w_in[half:, columns], preferred_element_type=jnp.float32
                )

            gate_act = project(gate_cols)
            up_act = project(up_cols)
            act = gate_act / (1.0 + jnp.exp(-gate_act)) * up_act
            hidden[:, gate_cols] = act.astype(jnp.bfloat16)
            return carry

        lax.fori_loop(0, 2 * unit // 256, hidden_tile, 0)
        for f in range(2):
            target = targets[f]

            def out_tile(j, carry, f=f, target=target):
                cols = pl.multiple_of(j * 512, 512)
                val = jnp.dot(
                    hidden[...], w_out[:, pl.ds(f * half + cols, 512)],
                    preferred_element_type=jnp.float32,
                )
                target[:, pl.ds(cols, 512)] = (val * weight).astype(target.dtype)
                return carry

            lax.fori_loop(0, half // 512, out_tile, 0)

    order = (3, 0, 2, 1)

    def leave_third(f, zz):
        return remote(
            leave.at[f, 0, piece(zz)], got_third.at[f, 0, piece(zz)],
            reduce_send.at[f, zz], reduce_recv.at[f, zz], third[f],
        )

    def leave_both(f, zz):
        return remote(
            leave.at[f, 1, piece(zz), left_cols], got_third.at[f, 1, piece(zz), left_cols],
            reduce_send.at[f, 4 + zz], reduce_recv.at[f, 4 + zz], third[f],
        )

    def leave_right(f):
        return remote(
            leave.at[f, 1, piece(z), right_cols], got_third.at[f, 1, piece(z), right_cols],
            reduce_send.at[f, 28], reduce_recv.at[f, 28], third[f],
        )

    def early_rising(f, zz):
        ref = early_rise.at[f, piece(zz)]
        return remote(ref, ref, reduce_send.at[f, 20 + zz], reduce_recv.at[f, 20 + zz], above)

    def early_falling(f, zz):
        ref = early_fall.at[f, piece(zz)]
        return remote(ref, ref, reduce_send.at[f, 24 + zz], reduce_recv.at[f, 24 + zz], below)

    def leave_second(f, zz):
        return remote(
            got_third.at[f, 1, piece(zz)], got_second.at[f, piece(zz)],
            reduce_send.at[f, 8 + zz], reduce_recv.at[f, 8 + zz], second[f],
        )

    def rising(f, zz):
        return remote(
            rise.at[f, piece(zz)], rise.at[f, piece(zz)],
            reduce_send.at[f, 12 + zz], reduce_recv.at[f, 12 + zz], above,
        )

    def falling(f, zz):
        return remote(
            fall.at[f, piece(zz)], fall.at[f, piece(zz)],
            reduce_send.at[f, 16 + zz], reduce_recv.at[f, 16 + zz], below,
        )

    relay_right(2)
    at_stage(3, relay_second)
    at_stage(2, send_third)
    at_stage(3, send_third)
    for local, swap in swaps:
        local.wait()
        swap.wait_recv()
    expert(0, 0, (stay.at[0], stay.at[1]))

    def wide(ref):
        return ref.astype(jnp.float32)

    def to_second(f, zz):
        def go():
            leave_both(f, zz).wait_recv()
            val = pass_on[f, piece(zz), left_cols] + wide(got_third[f, 1, piece(zz), left_cols])
            got_third[f, 1, piece(zz), left_cols] = val.astype(jnp.bfloat16)
            got_third[f, 1, piece(zz), right_cols] = pass_on[f, piece(zz), right_cols].astype(
                jnp.bfloat16
            )
            leave_second(f, zz).start()

        when(zz != z, go)

    def own_to_second(f):
        leave_both(f, z).wait_recv()
        leave_right(f).wait_recv()
        val = pass_on[f, piece(z), :] + wide(got_third[f, 1, piece(z), :])
        got_third[f, 1, piece(z), :] = val.astype(jnp.bfloat16)
        leave_second(f, z).start()

    def early_relay(buf, copy, zz):
        for f in range(2):
            copy(f, zz).wait_recv()
            val = wide(leave[f, 1, piece(zz), right_cols]) + wide(buf[f, piece(zz), :])
            buf[f, piece(zz), :] = val.astype(jnp.bfloat16)
            copy(f, zz).start()

    def early_up(zz):
        early_relay(early_rise, early_rising, zz)

    def early_down(zz):
        early_relay(early_fall, early_falling, zz)

    def early_first(buf, copy, pieces):
        for zz in pieces:
            for f in range(2):
                buf[f, piece(zz), :] = leave[f, 1, piece(zz), right_cols]
                copy(f, zz).start()

    def early_finish(up, down):
        for f in range(2):
            val = wide(leave[f, 1, piece(z), right_cols])
            if up:
                early_rising(f, z).wait_recv()
                val = val + wide(early_rise[f, piece(z), :])
            if down:
                early_falling(f, z).wait_recv()
                val = val + wide(early_fall[f, piece(z), :])
            leave[f, 1, piece(z), right_cols] = val.astype(jnp.bfloat16)
            leave_right(f).start()

    for zz in range(DEPTH):
        for f in range(2):
            second_third(f, zz).wait_recv()
    relay_right(3)
    expert(3, 3, (leave.at[0, 1], leave.at[1, 1]))
    for zz in order:
        for f in range(2):
            leave_both(f, zz).start()
    when(z == 0, lambda: early_first(early_rise, early_rising, (3, 2, 1)))
    when(z == DEPTH - 1, lambda: early_first(early_fall, early_falling, (0, 1, 2)))

    for zz in range(DEPTH):
        own_third(0, zz).wait_recv()
    expert(2, 1, (leave.at[0, 0], pass_on.at[1]))
    when(z == 1, lambda: early_up(3))
    when(z == 2, lambda: early_down(0))
    for zz in order[:2]:
        to_second(1, zz)
    for zz in order:
        leave_third(0, zz).start()
    for zz in range(DEPTH):
        own_third(1, zz).wait_recv()
    expert(1, 2, (pass_on.at[0], leave.at[1, 0]))
    when(z == 1, lambda: early_down(0))
    when(z == 2, lambda: early_up(3))
    for zz in order[:2]:
        to_second(0, zz)
    for zz in order:
        leave_third(1, zz).start()
    when(z == 1, lambda: early_up(2))
    when(z == 2, lambda: early_down(1))
    for zz in order[2:]:
        for f in range(2):
            to_second(f, zz)
    when(z == 0, lambda: early_finish(False, True))
    when(z == DEPTH - 1, lambda: early_finish(True, False))
    when(jnp.logical_not(edge), lambda: early_finish(True, True))

    def settle(zz):
        for f in range(2):
            leave_third(f, zz).wait_recv()
            leave_second(f, zz).wait_recv()
            stay[f, piece(zz), :] = (
                stay[f, piece(zz), :]
                + wide(got_third[f, 0, piece(zz), :])
                + wide(got_second[f, piece(zz), :])
            )

        def first_up():
            for f in range(2):
                rise[f, piece(zz), :] = stay[f, piece(zz), :].astype(jnp.bfloat16)
                rising(f, zz).start()

        def first_down():
            for f in range(2):
                fall[f, piece(zz), :] = stay[f, piece(zz), :].astype(jnp.bfloat16)
                falling(f, zz).start()

        if not isinstance(zz, int):
            return
        if zz > 0:
            when(z == 0, first_up)
        if zz < DEPTH - 1:
            when(z == DEPTH - 1, first_down)

    def relay_up(zz):
        for f in range(2):
            rising(f, zz).wait_recv()
            val = stay[f, piece(zz), :] + wide(rise[f, piece(zz), :])
            rise[f, piece(zz), :] = val.astype(jnp.bfloat16)
            rising(f, zz).start()

    def relay_down(zz):
        for f in range(2):
            falling(f, zz).wait_recv()
            val = stay[f, piece(zz), :] + wide(fall[f, piece(zz), :])
            fall[f, piece(zz), :] = val.astype(jnp.bfloat16)
            falling(f, zz).start()

    for i in range(1, DEPTH + 1):
        when(z != order[i - 1], lambda i=i: settle(order[i - 1]))
        if i == 2:
            for f in range(2):
                own_to_second(f)
            when(z == 1, lambda: relay_up(3))
            when(z == 2, lambda: relay_down(0))
        if i == 3:
            when(z == 1, lambda: relay_down(0))
            when(z == 2, lambda: relay_up(3))
    when(z == 1, lambda: relay_up(2))
    when(z == 2, lambda: relay_down(1))

    settle(z)
    cols = (pl.ds(0, half), pl.ds(half, half))

    def finish(up, down):
        for f in range(2):
            val = stay[f, piece(z), :]
            if up:
                rising(f, z).wait_recv()
                val = val + wide(rise[f, piece(z), :])
            if down:
                falling(f, z).wait_recv()
                val = val + wide(fall[f, piece(z), :])
            out_ref[:, cols[f]] = val.astype(out_ref.dtype)

    when(z == 0, lambda: finish(False, True))
    when(z == DEPTH - 1, lambda: finish(True, False))
    when(jnp.logical_not(edge), lambda: finish(True, True))

    for _, swap in swaps:
        swap.wait_send()
    for f in range(2):
        for zz in range(DEPTH):
            when(jnp.logical_and(z < DEPTH - 1, zz <= z), lambda f=f, zz=zz: climb(f, zz).wait_send())
            when(jnp.logical_and(z > 0, zz >= z), lambda f=f, zz=zz: sink(f, zz).wait_send())
            for copy in (own_second, own_third, second_third, leave_third, leave_both, leave_second):
                copy(f, zz).wait_send()
            when(zz > z, lambda f=f, zz=zz: rising(f, zz).wait_send())
            when(zz < z, lambda f=f, zz=zz: falling(f, zz).wait_send())
            when(zz > z, lambda f=f, zz=zz: early_rising(f, zz).wait_send())
            when(zz < z, lambda f=f, zz=zz: early_falling(f, zz).wait_send())
            when(jnp.logical_and(z < DEPTH - 1, zz <= z), lambda f=f, zz=zz: right_climb(f, zz).wait_send())
            when(jnp.logical_and(z > 0, zz >= z), lambda f=f, zz=zz: right_sink(f, zz).wait_send())
        right_third(f).wait_send()
        leave_right(f).wait_send()


def fused_body(tokens, routes, gate_probs, gate_w, up_w, down_w):
    experts = lax.axis_size("expert")
    tok, width = tokens.shape
    unit = gate_w.shape[2]
    half = width // 2
    line = DEPTH * tok
    expert_ids = jnp.arange(experts, dtype=jnp.int32)
    named = routes[:, :, None] == expert_ids
    spread = jnp.sum(jnp.where(named, gate_probs[:, :, None], 0.0), axis=1)
    coarse = lax.reduce_precision(spread, 8, 7)
    fine = spread - coarse
    tags = jnp.concatenate([coarse, fine], axis=1).astype(jnp.bfloat16)
    tags = jnp.pad(tags, ((0, 0), (0, TAG - 2 * experts)))
    vmem, anywhere = pl.BlockSpec(memory_space=pltpu.VMEM), pl.BlockSpec(memory_space=pl.ANY)
    bf16, f32, dma = jnp.bfloat16, jnp.float32, pltpu.SemaphoreType.DMA
    return pl.pallas_call(
        fused_kernel,
        out_shape=jax.ShapeDtypeStruct((tok, width), bf16),
        in_specs=[vmem, vmem, anywhere, anywhere, anywhere],
        out_specs=vmem,
        scratch_shapes=[
            pltpu.VMEM((4, line, TAG + half), bf16),
            pltpu.VMEM((4, line, half), bf16),
            pltpu.VMEM((width, 4 * unit), bf16),
            pltpu.VMEM((2 * unit, width), bf16),
            pltpu.VMEM((line, 2 * unit), bf16),
            pltpu.VMEM((2, line, half), f32),
            pltpu.VMEM((2, line, half), f32),
            pltpu.VMEM((2, 2, line, half), bf16),
            pltpu.VMEM((2, 2, line, half), bf16),
            pltpu.VMEM((2, line, half), bf16),
            pltpu.VMEM((2, line, half), bf16),
            pltpu.VMEM((2, line, half), bf16),
            pltpu.VMEM((2, line, half // 2), bf16),
            pltpu.VMEM((2, line, half // 2), bf16),
            dma((2, 29)),
            dma((2, 20)),
            dma((2, 29)),
            dma((2, 29)),
            dma((9,)),
        ],
        compiler_params=pltpu.CompilerParams(
            collective_id=0, has_side_effects=True, vmem_limit_bytes=60 * 2**20
        ),
        cost_estimate=pl.CostEstimate(
            flops=2 * experts * tok * width * unit * 6,
            bytes_accessed=6 * width * unit * 2,
            transcendentals=experts * tok * unit * 2,
        ),
    )(tokens, tags, gate_w[0], up_w[0], down_w[0])


def body(tokens, routes, *others):
    tok_count, top_count = routes.shape
    experts = lax.axis_size("expert")
    capacity = 2 * tok_count * top_count // experts
    if capacity >= tok_count and experts == 4 * DEPTH and lax.axis_size("dp") == 2:
        return fused_body(tokens, routes, *others)
    return exchange_body(tokens, routes, *others)


def solution(mesh):
    return jax.shard_map(
        body,
        mesh=mesh,
        in_specs=(
            P(("expert", "dp"), None),
            P(("expert", "dp"), None),
            P(("expert", "dp"), None),
            P("expert", None, "dp"),
            P("expert", None, "dp"),
            P("expert", "dp", None),
        ),
        out_specs=P(("expert", "dp"), None),
        check_vma=False,
    )
```
